128 devices in a mesh: lon: 8 (over z, x_hi), lat: 16 (over y, x_lo, core).
Axes of the slice: x: 4 (x_hi: 2, x_lo: 2; x = x_hi * 2 + x_lo), y: 4, z: 4, core: 2. Of those that a mesh axis runs over, the one named last changes fastest.
Arguments:
- state_field: bfloat16 [192, 128, 1024], P(None, 'lat', 'lon'), may hold values from -6 to 6
- depth_kernel: float32 [192, 49], replicated, may hold values from -0.875 to 0.875
- norm_gain: float32 [192], replicated, may hold values from 0.25 to 1.75
- w_expand: bfloat16 [192, 768], replicated, may hold values from -0.4375 to 0.4375
- w_project: bfloat16 [768, 192], replicated, may hold values from -0.21875 to 0.21875
- layer_scale: float32 [192], replicated, may hold values from 0.5 to 1.5
- cotangent: bfloat16 [192, 128, 1024], P(None, 'lat', 'lon'), may hold values from -6 to 6
- send_cells: int32 [16, 8192], P('lat', 'lon'), may hold values from 0 to 1023, as said below
- send_count: int32 [16, 128], P('lat', 'lon'), may hold values from 4 to 64, as said below
- fold_partner: int32 [1024], replicated, may hold values from 0 to 1023, each once
Outputs:
- out_field: bfloat16 [192, 128, 1024], P(None, 'lat', 'lon')
- grad_field: bfloat16 [192, 128, 1024], P(None, 'lat', 'lon')
- grad_kernel: float32 [192, 49], replicated
- grad_expand: float32 [192, 768], replicated
- grad_project: float32 [768, 192], replicated
The draws below stay inside these ranges and needn't reach their ends.
Inputs may be any that keep to these rules, and one draw needn't show every extreme that they name: `send_cells`: the entries of one device's row are distinct. `send_count`: A device has equally many live slots in every slot block. In every sector the devices of the 16 bands, in a drawn order, have 64 // 16 times 1, 2, ..., 16 live slots in each block.
All inputs are finite; a program needn't handle non-finite values.
Results may differ from the reference program's by a relative error of at most 0.0075.
Values may be sent and summed in bfloat16 or wider, within the bound.
A program may use at most 64 MiB of HBM per device.

```python
import jax
import jax.numpy as jnp
from jax import lax

CH = 192
HID = 768
TX = 128
TY = 8
BANDS = 16
SECTORS = 8
NLAT = 128
NLON = 1024
ROWS_DEV = 1024
CAP = 64


def pick_cells(subkey):
    return jax.random.permutation(subkey, TX * TY)[:ROWS_DEV]


def sector_order(subkey):
    return jax.random.permutation(subkey, BANDS)


def draw_send_cells(key, part):
    key = jax.random.fold_in(key, 11)
    subkeys = jax.random.split(key, BANDS * SECTORS)
    lists = jax.vmap(pick_cells)(subkeys)
    return lists.reshape(BANDS, SECTORS * ROWS_DEV).astype(jnp.int32)


def draw_send_count(key, part):
    key = jax.random.fold_in(key, 23)
    subkeys = jax.random.split(key, SECTORS)
    orders = jax.vmap(sector_order)(subkeys)
    levels = CAP // BANDS * (jnp.transpose(orders) + 1)
    counts = jnp.broadcast_to(levels[:, :, None], (BANDS, SECTORS, BANDS))
    return counts.reshape(BANDS, SECTORS * BANDS).astype(jnp.int32)


def shard_levels(key, extent, cuts, smallest, top_value):
    def one(dim, blocks):
        steps = jax.random.uniform(jax.random.fold_in(jax.random.fold_in(key, 6), dim), (blocks,), jnp.float32, smallest / len(cuts), top_value / len(cuts))
        return jnp.repeat(jnp.exp(steps), extent[dim] // blocks).reshape((-1,) + (1,) * (len(extent) - dim - 1))

    loudness = one(*cuts[0])
    for cut in cuts[1:]:
        loudness = loudness * one(*cut)
    return loudness


def noise(stream_key, shape, scale, bound, shards=(), kind=jnp.bfloat16):
    array = jax.random.normal(stream_key, shape, jnp.float32) * scale
    if len(shards) > 0:
        array = shard_levels(stream_key, shape, shards, -0.22, 0.18) * array
    return jnp.clip(array, min=-bound, max=bound).astype(kind)


def setup_inputs(seed: int = 0) -> dict:
    streams_of = jax.random.split(jax.random.key(seed), 11)
    return {
        "state_field": noise(streams_of[0], (CH, NLAT, NLON), 1.0, 6.0, ((1, 16), (2, 8))),
        "depth_kernel": noise(streams_of[1], (CH, 49), 49 ** -0.5, 0.875, (), jnp.float32),
        "norm_gain": jnp.clip(1.0 + 0.15 * jax.random.normal(streams_of[2], (CH,), jnp.float32), 0.25, 1.75),
        "w_expand": noise(streams_of[3], (CH, HID), CH ** -0.5, 0.4375),
        "w_project": noise(streams_of[4], (HID, CH), HID ** -0.5, 0.21875),
        "layer_scale": jnp.clip(jax.random.uniform(streams_of[5], (CH,), jnp.float32, 0.5, 1.5), 0.5, 1.5),
        "cotangent": noise(streams_of[6], (CH, NLAT, NLON), 1.0, 6.0, ((1, 16), (2, 8))),
        "send_cells": draw_send_cells(jax.random.fold_in(streams_of[10], 71), 0),
        "send_count": draw_send_count(jax.random.fold_in(streams_of[10], 71), 0),
        "fold_partner": jax.random.permutation(streams_of[9], NLON).astype(jnp.int32),
    }


root_half = 0.7071067811865476
root_twopi_inv = 0.3989422804014327

def gelu_value(pre_act):
    return 0.5 * pre_act * (1.0 + jax.scipy.special.erf(pre_act * root_half))

def gelu_slope(pre_act):
    return 0.5 * (1.0 + jax.scipy.special.erf(pre_act * root_half)) + pre_act * jnp.exp(-0.5 * pre_act * pre_act) * root_twopi_inv

def forward_rows(row_block, norm_gain, w_expand, w_project):
    values = row_block.astype(jnp.float32)
    center = values - lax.optimization_barrier(jnp.mean(values, axis=0, keepdims=True))
    variance = lax.optimization_barrier(jnp.mean(center * center, axis=0, keepdims=True))
    inv_std = lax.rsqrt(variance + 1e-06)
    normed = center * inv_std
    scaled = (normed * norm_gain[:, None]).astype(jnp.bfloat16)
    pre_act = lax.dot_general(w_expand, scaled, (((0,), (0,)), ((), ())), preferred_element_type=jnp.float32)
    hidden = gelu_value(pre_act).astype(jnp.bfloat16)
    output = lax.dot_general(w_project, hidden, (((0,), (0,)), ((), ())), preferred_element_type=jnp.float32)
    return (output.astype(jnp.bfloat16), (normed, inv_std, scaled, pre_act, hidden))

def backward_rows(stored, upstream, norm_gain, w_expand, w_project):
    normed, inv_std, scaled, pre_act, hidden = stored
    grad_hidden = jnp.dot(w_project, upstream, preferred_element_type=jnp.float32)
    grad_pre = (grad_hidden * gelu_slope(pre_act)).astype(jnp.bfloat16)
    grad_project = lax.dot_general(hidden, upstream, (((1,), (1,)), ((), ())), preferred_element_type=jnp.float32)
    grad_expand = lax.dot_general(scaled, grad_pre, (((1,), (1,)), ((), ())), preferred_element_type=jnp.float32)
    grad_scaled = jnp.dot(w_expand, grad_pre, preferred_element_type=jnp.float32)
    grad_normed = grad_scaled * norm_gain[:, None]
    grad_rows = inv_std * (grad_normed - lax.optimization_barrier(jnp.mean(grad_normed, axis=0, keepdims=True)) - normed * lax.optimization_barrier(jnp.mean(grad_normed * normed, axis=0, keepdims=True)))
    return (grad_rows.astype(jnp.bfloat16), grad_expand, grad_project)

def reference(state_field, depth_kernel, norm_gain, w_expand, w_project, layer_scale, cotangent, send_cells, send_count, fold_partner):
    ext_cols = ((jnp.arange(NLON + 6, dtype=jnp.int32) - 3) % NLON).astype(jnp.int32)
    wrapped = state_field[:, :, ext_cols]
    fold_cols = fold_partner[ext_cols]
    fold_rows = state_field[:, NLAT - 3:, :][:, ::-1, :][:, :, fold_cols]
    south_pad = jnp.zeros((CH, 3, NLON + 6), jnp.bfloat16)
    extended = jnp.concatenate([south_pad, wrapped, fold_rows], axis=1)
    ext_f32 = extended.astype(jnp.float32)
    convolved = jnp.zeros((CH, NLAT, NLON), jnp.float32)
    for row_off in range(7):
        for col_off in range(7):
            convolved = convolved + depth_kernel[:, 7 * row_off + col_off][:, None, None] * ext_f32[:, row_off:row_off + NLAT, col_off:col_off + NLON]
    rounded = convolved.astype(jnp.bfloat16).reshape(CH, NLAT * NLON)
    cell_table = send_cells.reshape(BANDS, SECTORS, ROWS_DEV)
    global_rows = jnp.arange(BANDS, dtype=jnp.int32)[:, None, None] * TY + cell_table // TX
    global_cols = jnp.arange(SECTORS, dtype=jnp.int32)[None, :, None] * TX + cell_table % TX
    flat_index = (global_rows * NLON + global_cols).reshape(BANDS * SECTORS, ROWS_DEV).astype(jnp.int32)
    counts = send_count.reshape(BANDS, SECTORS, BANDS)
    slot_block = (jnp.arange(ROWS_DEV, dtype=jnp.int32) // CAP).astype(jnp.int32)
    position = (jnp.arange(ROWS_DEV, dtype=jnp.int32) % CAP).astype(jnp.int32)
    live_mask = (position[None, None, :] < counts[:, :, slot_block]).reshape(BANDS * SECTORS, ROWS_DEV).astype(jnp.float32)
    cot_flat = cotangent.reshape(CH, NLAT * NLON)

    def per_device(totals, pieces):
        where_index, live_row = pieces
        row_block = jnp.take(rounded, where_index, axis=1)
        upstream = (live_row[None, :] * layer_scale[:, None] * jnp.take(cot_flat, where_index, axis=1).astype(jnp.float32)).astype(jnp.bfloat16)
        output, stored = forward_rows(row_block, norm_gain, w_expand, w_project)
        grad_rows, grad_expand, grad_project = backward_rows(stored, upstream, norm_gain, w_expand, w_project)
        return ((totals[0] + grad_expand, totals[1] + grad_project), (output, grad_rows))
    zero_grads = (jnp.zeros((CH, HID), jnp.float32), jnp.zeros((HID, CH), jnp.float32))
    (grad_expand, grad_project), (outputs, grad_rows) = lax.scan(per_device, zero_grads, (flat_index, live_mask))
    all_index = flat_index.reshape(-1)
    outputs = jnp.transpose(outputs, (1, 0, 2)).reshape(CH, -1)
    grad_rows = jnp.transpose(grad_rows, (1, 0, 2)).reshape(CH, -1)
    branch = live_mask.reshape(-1)[None, :] * layer_scale[:, None] * outputs.astype(jnp.float32)
    out_flat = state_field.reshape(CH, -1).astype(jnp.float32).at[:, all_index].add(branch)
    out_field = out_flat.astype(jnp.bfloat16).reshape(CH, NLAT, NLON)
    grad_conv = jnp.zeros((CH, NLAT * NLON), jnp.bfloat16).at[:, all_index].set(grad_rows).reshape(CH, NLAT, NLON)
    grad_wrapped = grad_conv[:, :, ext_cols]
    padded = jnp.concatenate([jnp.zeros((CH, 3, NLON + 6), jnp.bfloat16), grad_wrapped, jnp.zeros((CH, 6, NLON + 6), jnp.bfloat16)], axis=1).astype(jnp.float32)
    adjoint = jnp.zeros((CH, NLAT + 3, NLON), jnp.float32)
    for row_off in range(7):
        for col_off in range(7):
            adjoint = adjoint + depth_kernel[:, 7 * row_off + col_off][:, None, None] * padded[:, 6 - row_off:6 - row_off + NLAT + 3, 6 - col_off:6 - col_off + NLON]
    inverse = jnp.zeros((NLON,), jnp.int32).at[fold_partner].set(jnp.arange(NLON, dtype=jnp.int32))
    fold_term = adjoint[:, NLAT:NLAT + 3, :][:, :, inverse][:, ::-1, :]
    grad_f32 = cotangent.astype(jnp.float32) + adjoint[:, :NLAT, :]
    grad_f32 = grad_f32.at[:, NLAT - 3:, :].add(fold_term)
    grad_field = grad_f32.astype(jnp.bfloat16)
    grad_conv_f32 = grad_conv.astype(jnp.float32)
    kernel_terms = []
    for row_off in range(7):
        for col_off in range(7):
            kernel_terms.append(lax.optimization_barrier(jnp.sum(ext_f32[:, row_off:row_off + NLAT, col_off:col_off + NLON] * grad_conv_f32, axis=(1, 2))))
    grad_kernel = jnp.stack(kernel_terms, axis=1)
    return (out_field, grad_field, grad_kernel, grad_expand, grad_project)
```

```python
import functools

import jax
import jax.numpy as jnp
from jax import lax
from jax.experimental import pallas as pl
from jax.experimental.pallas import tpu as pltpu
from jax.sharding import PartitionSpec as P

MESH = pl.DeviceIdType.MESH
F32 = jnp.float32
BF16 = jnp.bfloat16
ROOT_HALF = 0.7071067811865476
ROOT_TWOPI_INV = 0.3989422804014327

C = 192
HID = 768
TY = 8
TX = 128
EXT = TY + 6
CELLS = TY * TX
TAPS = 49
GROUPS = 4
GC = C // GROUPS
WROWS = 2 * C * HID // 128
KROWS = 256
PIECE = 48


def dot_nn(a, b):
    return jnp.dot(a, b, preferred_element_type=F32)


def dot_nt(a, b):
    return lax.dot_general(a, b, (((1,), (1,)), ((), ())), preferred_element_type=F32)


def wait_bytes(ref, sem):
    pltpu.make_async_copy(ref, ref, sem).wait()


def column(row_ref):
    n = row_ref.shape[1]
    eye = lax.broadcasted_iota(jnp.int32, (n, n), 0) == lax.broadcasted_iota(
        jnp.int32, (n, n), 1
    )
    return jnp.sum(jnp.where(eye, row_ref[...], 0.0), axis=1, keepdims=True)


def pack_edges(rows, west, east):
    lane = lax.broadcasted_iota(jnp.int32, (GC, 128), 1)
    w = jnp.zeros((GC, 128), F32)
    e = jnp.zeros((GC, 128), F32)
    for q in range(GROUPS):
        for j in range(TY):
            at = 32 * q + 4 * j
            x = rows[3 + j, q * GC : (q + 1) * GC, :]
            slot = (lane >= at) & (lane < at + 4)
            w = jnp.where(slot, pltpu.roll(x, at, 1) if at else x, w)
            e = jnp.where(slot, pltpu.roll(x, (at + 4) % 128, 1), e)
    west[...] = w.astype(BF16)
    east[...] = e.astype(BF16)


def unpack_edges(edges, halo):
    lane = lax.broadcasted_iota(jnp.int32, (GC, 128), 1)
    for part, (r0, r1, j0) in enumerate(((0, 3, 5), (3, 11, 0), (11, 14, 0))):
        left = edges[part].astype(F32)
        right = edges[3 + part].astype(F32)
        for r in range(r0, r1):
            j = r - r0 + j0
            for q in range(GROUPS):
                at = 32 * q + 4 * j
                lf = pltpu.roll(left, (124 - at) % 128, 1) if at != 124 else left
                rt = pltpu.roll(right, (128 - at) % 128, 1) if at else right
                halo[r, q * GC : (q + 1) * GC, :] = jnp.where(lane < 64, rt, lf)


def shifted_rows(rows, halo, c0, r0, r1, d, lane):
    sh = d - 3
    x = rows[r0:r1, pl.ds(c0, 8), :]
    if sh == 0:
        return x
    h = halo[r0:r1, pl.ds(c0, 8), :]
    m = (lane < sh) if sh > 0 else (lane >= 128 + sh)
    return pltpu.roll(jnp.where(m, h, x), (-sh) % 128, 2)


def conv_tile(rows, halo, dk, c0, reverse):
    lane = lax.broadcasted_iota(jnp.int32, (EXT, 8, 128), 2)
    kv = dk[pl.ds(c0, 8), :]
    acc = jnp.zeros((TY, 8, 128), F32)
    for d in range(7):
        x = shifted_rows(rows, halo, c0, 0, EXT, d, lane)
        for a in range(7):
            t = 7 * a + d
            if reverse:
                t = TAPS - 1 - t
            acc = acc + kv[:, t : t + 1][None] * x[a : a + TY]
    return acc


def block_kernel(
    bands,
    sectors,
    state,
    cot,
    dk,
    gain,
    lscale,
    w_expand,
    w_project,
    cells,
    counts,
    partner,
    out_rows,
    grad_rows,
    sums_out,
    nat,
    ext,
    halo,
    gext,
    ghalo,
    cotr,
    conv,
    upstream,
    scaled,
    hidden,
    gradpre,
    wexpt,
    wprojt,
    wet,
    dkp,
    gk,
    sendrows,
    sendedge,
    recvrows,
    recvedge,
    gsendrows,
    gsendedge,
    grecvrows,
    grecvedge,
    foldrecv,
    foldsend2,
    foldrecv2,
    onehot,
    part,
    partrecv,
    total,
    totalrecv,
    full,
    final,
    sems,
):
    wch = WROWS // bands
    kch = KROWS // bands
    chunk = wch + kch
    piece = totalrecv.shape[1]
    lat = lax.axis_index("lat")
    lon = lax.axis_index("lon")
    is_south = lat == 0
    is_north = lat == bands - 1

    def peer(dlat, dlon):
        return {
            "lat": lax.rem(lat + (dlat + bands), bands),
            "lon": lax.rem(lon + (dlon + sectors), sectors),
        }

    def send(src, dst, s, device):
        cp = pltpu.make_async_remote_copy(
            src_ref=src,
            dst_ref=dst,
            send_sem=sems.at[2 * s],
            recv_sem=sems.at[2 * s + 1],
            device_id=device,
            device_id_type=MESH,
        )
        cp.start()

    barrier = pltpu.get_barrier_semaphore()
    peers = [(o, 0) for o in range(1, bands)] + [(0, o) for o in range(1, sectors)]
    peers += [(1, 1), (1, -1), (-1, 1), (-1, -1)]
    for dlat, dlon in peers:
        pl.semaphore_signal(barrier, inc=1, device_id=peer(dlat, dlon), device_id_type=MESH)

    nat[...] = state[...].astype(F32)
    for j in range(TY):
        ext[3 + j] = nat[pl.ds(j, C, stride=TY), :]
    for k, j in enumerate((0, 1, 2, 5, 6, 7)):
        sendrows[k * C : (k + 1) * C, :] = ext[3 + j].astype(BF16)
    pack_edges(ext, sendedge.at[0], sendedge.at[1])

    pl.semaphore_wait(barrier, len(peers))

    def exchange(rows_s, edge_s, rows_r, edge_r, s):
        send(rows_s.at[pl.ds(0, 3 * C)], rows_r.at[pl.ds(3 * C, 3 * C)], s, peer(-1, 0))
        send(rows_s.at[pl.ds(3 * C, 3 * C)], rows_r.at[pl.ds(0, 3 * C)], s, peer(1, 0))
        for n, dlat in enumerate((1, 0, -1)):
            send(edge_s.at[1], edge_r.at[n], s + 1, peer(dlat, 1))
            send(edge_s.at[0], edge_r.at[3 + n], s + 1, peer(dlat, -1))

    @pl.when(is_north)
    def _():
        for o in range(1, sectors):
            send(
                sendrows.at[pl.ds(3 * C, 3 * C)],
                foldrecv.at[pl.ds(lon * (3 * C), 3 * C)],
                2,
                peer(0, o),
            )

    exchange(sendrows, sendedge, recvrows, recvedge, 0)

    seg = lax.broadcasted_iota(jnp.int32, (1, CELLS), 1)
    capacity = CELLS // bands
    filled = jnp.zeros((1, CELLS), jnp.int32)
    for p in range(bands):
        filled = jnp.where(seg // capacity == p, counts[0, p], filled)
    live = (seg % capacity) < filled
    row_of = jnp.right_shift(cells[...], 7)
    col_of = jnp.bitwise_and(cells[...], 127)
    in_row = (lax.broadcasted_iota(jnp.int32, (TY, CELLS), 0) == row_of) & live
    in_col = lax.broadcasted_iota(jnp.int32, (TX, CELLS), 0) == col_of
    wet[...] = dot_nt(
        jnp.where(in_row, 1.0, 0.0).astype(BF16), jnp.where(in_col, 1.0, 0.0).astype(BF16)
    )
    gain_c = column(gain)
    scale_c = column(lscale)
    nat[...] = cot[...].astype(F32)
    for j in range(TY):
        x = nat[pl.ds(j, C, stride=TY), :]
        cotr[j] = x
        upstream[:, j * TX : (j + 1) * TX] = (wet[j : j + 1, :] * scale_c * x).astype(BF16)
    wexpt[...] = w_expand[...].astype(F32).T.astype(BF16)
    wprojt[...] = w_project[...].astype(F32).T.astype(BF16)
    dkp[...] = jnp.zeros((C, 128), F32)
    dkp[:, :TAPS] = dk[...]
    gk[C:, :] = jnp.zeros((KROWS - C, 128), F32)

    left = lax.rem(lon + sectors - 1, sectors)
    right = lax.rem(lon + 1, sectors)

    @pl.when(is_north)
    def _():
        mine = partner[pl.ds(lon, 1), :]
        lane = lax.broadcasted_iota(jnp.int32, (1, TX), 1)
        near = jnp.where(lane < 64, partner[pl.ds(right, 1), :], partner[pl.ds(left, 1), :])
        wanted = jnp.concatenate([mine, near], axis=1)
        for s in range(sectors):
            col = lax.broadcasted_iota(jnp.int32, (TX, 2 * TX), 0) + s * TX
            onehot[s] = jnp.where(col == wanted, 1.0, 0.0).astype(BF16)
        foldrecv[pl.ds(lon * (3 * C), 3 * C), :] = sendrows[3 * C :, :]

    def fill_halo(rows_r, edge_r, rows, hal, s):
        wait_bytes(rows_r, sems.at[2 * s + 1])
        wait_bytes(edge_r, sems.at[2 * s + 3])
        for k in range(3):
            rows[k] = jnp.where(is_south, 0.0, rows_r[k * C : (k + 1) * C, :].astype(F32))
            rows[11 + k] = jnp.where(
                is_north, 0.0, rows_r[(3 + k) * C : (4 + k) * C, :].astype(F32)
            )
        unpack_edges(edge_r, hal)

        @pl.when(is_south)
        def _():
            hal[0:3] = jnp.zeros((3, C, 128), F32)

        @pl.when(is_north)
        def _():
            hal[11:14] = jnp.zeros((3, C, 128), F32)

    fill_halo(recvrows, recvedge, ext, halo, 0)

    @pl.when(is_north)
    def _():
        wait_bytes(foldrecv.at[pl.ds(0, (sectors - 1) * 3 * C)], sems.at[5])
        for k in range(3):
            acc = jnp.zeros((C, 2 * TX), F32)
            for s in range(sectors):
                base = s * 3 * C + (2 - k) * C
                acc = acc + dot_nn(foldrecv[base : base + C, :], onehot[s])
            ext[11 + k] = acc[:, :TX]
            halo[11 + k] = acc[:, TX:]

    def conv_body(ct, carry):
        c0 = pl.multiple_of(ct * 8, 8)
        acc = conv_tile(ext, halo, dkp, c0, False)
        conv[:, pl.ds(c0, 8), :] = acc.astype(BF16).astype(F32)
        return carry

    lax.fori_loop(0, C // 8, conv_body, 0)

    def mlp_body(m, carry):
        at = pl.ds(pl.multiple_of(m * 256, 256), 256)
        v = jnp.concatenate([conv[2 * m], conv[2 * m + 1]], axis=1)
        center = v - jnp.mean(v, axis=0, keepdims=True)
        variance = jnp.mean(center * center, axis=0, keepdims=True)
        inv_std = lax.rsqrt(variance + 1e-06)
        normed = center * inv_std
        sc = (normed * gain_c).astype(BF16)
        scaled[:, at] = sc
        up = upstream[:, at]
        for h in range(0, HID, 256):
            pre = dot_nn(wexpt[h : h + 256, :], sc)
            gh = dot_nn(w_project[h : h + 256, :], up)
            half = 0.5 * (1.0 + lax.erf(pre * ROOT_HALF))
            hidden[h : h + 256, at] = (pre * half).astype(BF16)
            slope = half + pre * jnp.exp(-0.5 * pre * pre) * ROOT_TWOPI_INV
            gradpre[h : h + 256, at] = (gh * slope).astype(BF16)
        branch = dot_nn(wprojt[...], hidden[:, at]).astype(BF16).astype(F32)
        gs = dot_nn(w_expand[...], gradpre[:, at]) * gain_c
        gr = inv_std * (
            gs
            - jnp.mean(gs, axis=0, keepdims=True)
            - normed * jnp.mean(gs * normed, axis=0, keepdims=True)
        )
        gr = gr.astype(BF16).astype(F32)
        for n in range(2):
            half_at = slice(n * TX, (n + 1) * TX)
            j = 2 * m + n
            b = wet[pl.ds(j, 1), :] * scale_c * branch[:, half_at]
            out_rows[j] = (ext[3 + j] + b).astype(BF16)
            gext[3 + j] = gr[:, half_at]
        return carry

    lax.fori_loop(0, TY // 2, mlp_body, 0)

    for k, j in enumerate((0, 1, 2, 5, 6, 7)):
        gsendrows[k * C : (k + 1) * C, :] = gext[3 + j].astype(BF16)
    pack_edges(gext, gsendedge.at[0], gsendedge.at[1])
    exchange(gsendrows, gsendedge, grecvrows, grecvedge, 3)

    def gk_body(ct, carry):
        c0 = pl.multiple_of(ct * 8, 8)
        lane = lax.broadcasted_iota(jnp.int32, (EXT, 8, 128), 2)
        g = gext[3 : 3 + TY, pl.ds(c0, 8), :]
        res = jnp.zeros((8, 128), F32)
        for d in range(7):
            x = shifted_rows(ext, halo, c0, 0, EXT, d, lane)
            for a in range(7):
                s = jnp.sum(x[a : a + TY] * g, axis=0)
                res = jnp.where(lane[0] == 7 * a + d, jnp.sum(s, axis=1, keepdims=True), res)
        gk[pl.ds(c0, 8), :] = res
        return carry

    lax.fori_loop(0, C // 8, gk_body, 0)

    def put(w, value):
        part[(w // wch) * chunk + w % wch : (w // wch) * chunk + w % wch + PIECE, :] = value

    ge = dot_nt(scaled[...], gradpre[...])
    for b in range(HID // 128):
        for r in range(0, C, PIECE):
            put(b * C + r, ge[r : r + PIECE, b * 128 : (b + 1) * 128].astype(BF16))
    gp = dot_nt(hidden[...], upstream[...])
    base = C * HID // 128
    for r in range(0, HID, PIECE):
        put(base + r, gp[r : r + PIECE, :128].astype(BF16))
    hh = HID // 2
    for r in range(0, hh, PIECE):
        value = jnp.concatenate(
            [gp[r : r + PIECE, 128:], gp[hh + r : hh + r + PIECE, 128:]], axis=1
        )
        put(base + HID + r, value.astype(BF16))
    for p in range(bands):
        value = gk[p * kch : (p + 1) * kch, :].astype(BF16)
        part[p * chunk + wch : (p + 1) * chunk, :] = value

    for o in range(1, bands):
        to = peer(o, 0)
        send(part.at[pl.ds(to["lat"] * chunk, chunk)], partrecv.at[o - 1], 5, to)

    fill_halo(grecvrows, grecvedge, gext, ghalo, 3)

    @pl.when(is_north)
    def _():
        def fold_body(ct, carry):
            c0 = pl.multiple_of(ct * 8, 8)
            lane = lax.broadcasted_iota(jnp.int32, (3, 8, 128), 2)
            kv = dkp[pl.ds(c0, 8), :]
            acc = [jnp.zeros((8, 128), F32) for _ in range(3)]
            for d in range(7):
                x = shifted_rows(gext, ghalo, c0, 8, 11, d, lane)
                for k in range(3):
                    for a in range(3 - k):
                        t = TAPS - 1 - (7 * a + d)
                        acc[k] = acc[k] + kv[:, t : t + 1] * x[k + a]
            for k in range(3):
                ghalo[11 + k, pl.ds(c0, 8), :] = acc[k]
            return carry

        lax.fori_loop(0, C // 8, fold_body, 0)
        for k in range(3):
            foldsend2[k * C : (k + 1) * C, :] = ghalo[11 + k].astype(BF16)
            ghalo[11 + k] = jnp.zeros((C, 128), F32)
        for o in range(1, sectors):
            send(
                foldsend2,
                foldrecv2.at[pl.ds(lon * (3 * C), 3 * C)],
                6,
                peer(0, o),
            )

    def adj_body(ct, carry):
        c0 = pl.multiple_of(ct * 8, 8)
        acc = conv_tile(gext, ghalo, dkp, c0, True)
        conv[:, pl.ds(c0, 8), :] = acc + cotr[:, pl.ds(c0, 8), :]
        return carry

    lax.fori_loop(0, C // 8, adj_body, 0)

    wait_bytes(partrecv, sems.at[11])
    own = part[pl.ds(pl.multiple_of(lat * chunk, 16), chunk), :].astype(F32)
    for o in range(1, bands):
        own = own + partrecv[o - 1].astype(F32)
    total[0:chunk, :] = own
    if total.shape[0] > chunk:
        total[chunk:, :] = jnp.zeros((total.shape[0] - chunk, 128), F32)
    for o in range(1, sectors):
        to = peer(0, o)
        send(total.at[pl.ds(to["lon"] * piece, piece)], totalrecv.at[o - 1], 7, to)
    mine = pl.ds(pl.multiple_of(lon * piece, 8), piece)
    acc = total[mine, :]
    wait_bytes(totalrecv, sems.at[15])
    for o in range(1, sectors):
        acc = acc + totalrecv[o - 1]
    full[mine, :] = acc
    for o in range(1, sectors):
        send(full.at[pl.ds(lon * piece, piece)], full.at[pl.ds(lon * piece, piece)], 8, peer(0, o))
    wait_bytes(full.at[pl.ds(0, (sectors - 1) * piece)], sems.at[17])
    mine = pl.ds(pl.multiple_of(lat * chunk, 16), chunk)
    final[mine, :] = full[0:chunk, :].astype(BF16)
    for o in range(1, bands):
        send(final.at[pl.ds(lat * chunk, chunk)], final.at[pl.ds(lat * chunk, chunk)], 9, peer(o, 0))

    @pl.when(is_north)
    def _():
        foldrecv2[pl.ds(lon * (3 * C), 3 * C), :] = foldsend2[...]
        wait_bytes(foldrecv2.at[pl.ds(0, (sectors - 1) * 3 * C)], sems.at[13])
        col = lax.broadcasted_iota(jnp.int32, (TX, TX), 0) + lon * TX
        for k in range(3):
            acc = jnp.zeros((C, TX), F32)
            for s in range(sectors):
                here = jnp.where(partner[s : s + 1, :] == col, 1.0, 0.0).astype(BF16)
                base = s * 3 * C + k * C
                acc = acc + dot_nt(foldrecv2[base : base + C, :], here)
            conv[7 - k] = conv[7 - k] + acc

    for j in range(TY):
        grad_rows[j] = conv[j].astype(BF16)

    wait_bytes(final.at[pl.ds(0, (bands - 1) * chunk)], sems.at[19])
    sums_out[...] = final[...]

    wait_bytes(recvrows, sems.at[0])
    wait_bytes(recvedge, sems.at[2])
    wait_bytes(grecvrows, sems.at[6])
    wait_bytes(grecvedge, sems.at[8])
    wait_bytes(partrecv, sems.at[10])
    wait_bytes(totalrecv, sems.at[14])
    wait_bytes(totalrecv, sems.at[16])
    wait_bytes(final.at[pl.ds(0, (bands - 1) * chunk)], sems.at[18])

    @pl.when(is_north)
    def _():
        wait_bytes(foldrecv.at[pl.ds(0, (sectors - 1) * 3 * C)], sems.at[4])
        wait_bytes(foldrecv2.at[pl.ds(0, (sectors - 1) * 3 * C)], sems.at[12])


def finish_kernel(
    bands, out_rows, grad_rows, sums, out_field, grad_field, gk, ge, gp, nat
):
    wch = WROWS // bands
    kch = KROWS // bands
    chunk = wch + kch
    for src, dst in ((out_rows, out_field), (grad_rows, grad_field)):
        for j in range(TY):
            nat[pl.ds(j, C, stride=TY), :] = src[j].astype(F32)
        dst[...] = nat[...].astype(BF16)

    def get(w):
        at = (w // wch) * chunk + w % wch
        return sums[at : at + PIECE, :].astype(F32)

    for b in range(HID // 128):
        for r in range(0, C, PIECE):
            ge[r : r + PIECE, b * 128 : (b + 1) * 128] = get(b * C + r)
    base = C * HID // 128
    hh = HID // 2
    for r in range(0, HID, PIECE):
        gp[r : r + PIECE, :128] = get(base + r)
    for r in range(0, hh, PIECE):
        x = get(base + HID + r)
        gp[r : r + PIECE, 128:] = x[:, : C - 128]
        gp[hh + r : hh + r + PIECE, 128:] = x[:, C - 128 :]
    for r in range(0, C, 16):
        at = (r // kch) * chunk + wch + r % kch
        gk[r : r + 16, :] = sums[at : at + 16, :TAPS].astype(F32)


def on_device(
    bands,
    sectors,
    state_field,
    depth_kernel,
    norm_gain,
    w_expand,
    w_project,
    layer_scale,
    cotangent,
    send_cells,
    send_count,
    fold_partner,
):
    chunk = (WROWS + KROWS) // bands
    piece = -(-chunk // (8 * sectors)) * 8
    vmem = pl.BlockSpec(memory_space=pltpu.VMEM)
    smem = pl.BlockSpec(memory_space=pltpu.SMEM)
    sds = jax.ShapeDtypeStruct
    rows3 = pltpu.VMEM((6 * C, 128), BF16)
    edge = pltpu.VMEM((6, GC, 128), BF16)
    fold = pltpu.VMEM((sectors * 3 * C, 128), BF16)
    scratch = dict(
        nat=pltpu.VMEM((C * TY, 128), F32),
        ext=pltpu.VMEM((EXT, C, 128), F32),
        halo=pltpu.VMEM((EXT, C, 128), F32),
        gext=pltpu.VMEM((EXT, C, 128), F32),
        ghalo=pltpu.VMEM((EXT, C, 128), F32),
        cotr=pltpu.VMEM((TY, C, 128), F32),
        conv=pltpu.VMEM((TY, C, 128), F32),
        upstream=pltpu.VMEM((C, CELLS), BF16),
        scaled=pltpu.VMEM((C, CELLS), BF16),
        hidden=pltpu.VMEM((HID, CELLS), BF16),
        gradpre=pltpu.VMEM((HID, CELLS), BF16),
        wexpt=pltpu.VMEM((HID, C), BF16),
        wprojt=pltpu.VMEM((C, HID), BF16),
        wet=pltpu.VMEM((TY, TX), F32),
        dkp=pltpu.VMEM((C, 128), F32),
        gk=pltpu.VMEM((KROWS, 128), F32),
        sendrows=rows3,
        sendedge=pltpu.VMEM((2, GC, 128), BF16),
        recvrows=rows3,
        recvedge=edge,
        gsendrows=rows3,
        gsendedge=pltpu.VMEM((2, GC, 128), BF16),
        grecvrows=rows3,
        grecvedge=edge,
        foldrecv=fold,
        foldsend2=pltpu.VMEM((3 * C, 128), BF16),
        foldrecv2=fold,
        onehot=pltpu.VMEM((sectors, TX, 2 * TX), BF16),
        part=pltpu.VMEM((bands * chunk, 128), BF16),
        partrecv=pltpu.VMEM((bands - 1, chunk, 128), BF16),
        total=pltpu.VMEM((sectors * piece, 128), F32),
        totalrecv=pltpu.VMEM((sectors - 1, piece, 128), F32),
        full=pltpu.VMEM((sectors * piece, 128), F32),
        final=pltpu.VMEM((bands * chunk, 128), BF16),
        sems=pltpu.SemaphoreType.DMA((20,)),
    )
    out_rows, grad_rows, sums = pl.pallas_call(
        functools.partial(block_kernel, bands, sectors),
        out_shape=(
            sds((TY, C, 128), BF16),
            sds((TY, C, 128), BF16),
            sds((bands * chunk, 128), BF16),
        ),
        in_specs=[vmem] * 8 + [smem] + [vmem],
        out_specs=(vmem, vmem, vmem),
        scratch_shapes=list(scratch.values()),
        compiler_params=pltpu.CompilerParams(
            collective_id=0, has_side_effects=True, vmem_limit_bytes=48 * 2**20
        ),
        name="block",
    )(
        state_field.reshape(C * TY, TX),
        cotangent.reshape(C * TY, TX),
        depth_kernel,
        norm_gain.reshape(1, C),
        layer_scale.reshape(1, C),
        w_expand,
        w_project,
        send_cells,
        send_count,
        fold_partner.reshape(sectors, TX),
    )
    out_field, grad_field, gk, ge, gp = pl.pallas_call(
        functools.partial(finish_kernel, bands),
        out_shape=(
            sds((C * TY, TX), BF16),
            sds((C * TY, TX), BF16),
            sds((C, TAPS), F32),
            sds((C, HID), F32),
            sds((HID, C), F32),
        ),
        in_specs=[vmem] * 3,
        out_specs=(vmem,) * 5,
        scratch_shapes=[pltpu.VMEM((C * TY, 128), F32)],
        compiler_params=pltpu.CompilerParams(vmem_limit_bytes=32 * 2**20),
        name="finish",
    )(out_rows, grad_rows, sums)
    return (
        out_field.reshape(C, TY, TX),
        grad_field.reshape(C, TY, TX),
        gk,
        ge,
        gp,
    )


def solution(mesh):
    return jax.shard_map(
        functools.partial(on_device, mesh.shape["lat"], mesh.shape["lon"]),
        mesh=mesh,
        in_specs=(
            P(None, "lat", "lon"),
            P(),
            P(),
            P(),
            P(),
            P(),
            P(None, "lat", "lon"),
            P("lat", "lon"),
            P("lat", "lon"),
            P(),
        ),
        out_specs=(P(None, "lat", "lon"), P(None, "lat", "lon"), P(), P(), P()),
        check_vma=False,
    )
```

```python
import functools

import jax
import jax.numpy as jnp
from jax import lax
from jax.experimental import pallas as pl
from jax.experimental.pallas import tpu as pltpu
from jax.sharding import PartitionSpec as P

MESH = pl.DeviceIdType.MESH
F32 = jnp.float32
BF16 = jnp.bfloat16
ROOT_HALF = 0.7071067811865476
ROOT_TWOPI_INV = 0.3989422804014327

C = 192
HID = 768
TY = 8
TX = 128
EXT = TY + 6
CELLS = TY * TX
TAPS = 49
GROUPS = 4
GC = C // GROUPS
WROWS = 2 * C * HID // 128
PIECE = 96


def dot_nn(a, b):
    return jnp.dot(a, b, preferred_element_type=F32)


def dot_nt(a, b):
    return lax.dot_general(a, b, (((1,), (1,)), ((), ())), preferred_element_type=F32)


def wait_bytes(ref, sem):
    pltpu.make_async_copy(ref, ref, sem).wait()


def column(row_ref):
    n = row_ref.shape[1]
    eye = lax.broadcasted_iota(jnp.int32, (n, n), 0) == lax.broadcasted_iota(
        jnp.int32, (n, n), 1
    )
    return jnp.sum(jnp.where(eye, row_ref[...], 0.0), axis=1, keepdims=True)


def slot_lanes(shape, base, n):
    lane = lax.broadcasted_iota(jnp.int32, shape, len(shape) - 1)
    return (lane >= base) & (lane < base + n)


def turn(x, shift):
    shift %= 128
    return pltpu.roll(x, shift, x.ndim - 1) if shift else x


def pack_edges(rows, packed):
    shape = (GC, 128)
    for q in range(GROUPS):
        at = slice(q * GC, (q + 1) * GC)
        p = jnp.zeros(shape, F32)
        for j in range(TY):
            x = rows[3 + j, at, :]
            p = jnp.where(slot_lanes(shape, 4 * j, 3), turn(x, 4 * j), p)
            p = jnp.where(slot_lanes(shape, 64 + 4 * j, 3), turn(x, 64 + 4 * j - 125), p)
        packed[at, :] = p


def edge_messages(packed, west, east):
    shape = (GC, 128)
    w = packed[0:GC, :]
    e = turn(w, 64)
    for q in range(1, GROUPS):
        x = packed[q * GC : (q + 1) * GC, :]
        here = slot_lanes(shape, 32 * q, 32)
        w = jnp.where(here, turn(x, 32 * q), w)
        e = jnp.where(here, turn(x, 32 * q - 64), e)
    west[...] = w.astype(BF16)
    east[...] = e.astype(BF16)


def unpack_edges(msgs, edge, is_south, is_north):
    shape = (GC, 128)
    lane = lax.broadcasted_iota(jnp.int32, shape, 1)
    within = jnp.bitwise_and(lane, 63)
    dead = (is_south & (within < 12)) | (is_north & (within >= 44))
    values = [msgs[n].astype(F32) for n in range(6)]
    for q in range(GROUPS):
        p = jnp.zeros(shape, F32)
        for side in range(2):
            for n, (at, width, j0) in enumerate(((0, 12, 5), (12, 32, 0), (44, 12, 0))):
                to = 64 * side + at
                x = turn(values[3 * side + n], to - 32 * q - 4 * j0)
                p = jnp.where(slot_lanes(shape, to, width), x, p)
        edge[q * GC : (q + 1) * GC, :] = jnp.where(dead, 0.0, p)


def shifted(x, d):
    sh = d - 3
    if sh == 0:
        return x
    lane = lax.broadcasted_iota(jnp.int32, x.shape, x.ndim - 1)
    x = jnp.where((lane >= sh) if sh > 0 else (lane < 128 + sh), x, 0.0)
    return turn(x, -sh)


def tap(a, d, reverse):
    t = 7 * a + d
    return TAPS - 1 - t if reverse else t


def conv_own(rows, kb, cs, reverse, acc):
    x = rows[3 : 3 + TY, cs, :]
    for d in range(7):
        y = shifted(x, d)
        for a in range(7):
            k = kb[tap(a, d, reverse), cs, :]
            for j in range(max(0, 3 - a), min(TY, 11 - a)):
                acc[j] = acc[j] + k * y[j + a - 3]
    return acc


def edge_terms(edge, cs):
    shape = (cs.size, 128)
    lane = lax.broadcasted_iota(jnp.int32, shape, 1)
    within = jnp.bitwise_and(lane, 3)
    left = lane < 64
    e = edge[cs, :]
    terms = [jnp.where(within < 3, e, 0.0)]
    for s in (1, 2):
        lf = jnp.where(left & (within <= 2 - s), turn(e, -s), 0.0)
        terms.append(
            jnp.where((lane >= 64) & (within >= s) & (within < 3), turn(e, s), lf)
        )
    return terms


def edge_sums(edge, kb, cs, reverse, depth):
    left = slot_lanes((cs.size, 128), 0, 64)
    terms = edge_terms(edge, cs)
    total = None
    for a in range(depth):
        y = None
        for s in range(3):
            lf = kb[tap(a, s, reverse), cs, :]
            rt = kb[tap(a, 6 - s, reverse), cs, :]
            k = jnp.where(left, lf, rt)
            y = k * terms[s] if y is None else y + k * terms[s]
        y = turn(y, -4 * a)
        total = y if total is None else total + y
    return total


def edge_row(total, j):
    west = jnp.where(slot_lanes(total.shape, 0, 3), turn(total, -4 * j), 0.0)
    return jnp.where(slot_lanes(total.shape, 125, 3), turn(total, 61 - 4 * j), west)


def conv_halo(rows, kb, cs, reverse, acc, south, north):
    if south:
        lo_rows = rows[0:3, cs, :]
    if north:
        hi_rows = rows[3 + TY :, cs, :]
    for d in range(7):
        if south:
            lo = shifted(lo_rows, d)
            for a in range(3):
                k = kb[tap(a, d, reverse), cs, :]
                for r in range(a, 3):
                    acc[r - a] = acc[r - a] + k * lo[r]
        if north:
            hi = shifted(hi_rows, d)
            for a in range(4, 7):
                k = kb[tap(a, d, reverse), cs, :]
                for r in range(0, a - 3):
                    acc[11 + r - a] = acc[11 + r - a] + k * hi[r]
    return acc


def conv_edge(edge, kb, cs, reverse, acc, first):
    total = edge_sums(edge, kb, cs, reverse, 7)
    for j in range(first, TY):
        acc[j] = acc[j] + edge_row(total, j)
    return acc


def block_kernel(
    bands,
    sectors,
    state,
    cot,
    dkt,
    gain,
    lscale,
    w_expand,
    wprojt,
    cells,
    counts,
    partner,
    out_rows,
    grad_rows,
    sums_out,
    nat,
    ext,
    gext,
    edge,
    gedge,
    packed,
    gpacked,
    cotr,
    conv,
    upstream,
    scaled,
    hidden,
    gradpre,
    wexpt,
    w_project,
    wet,
    kb,
    fedge,
    gk,
    sendrows,
    sendedge,
    recvrows,
    recvedge,
    gsendrows,
    gsendedge,
    grecvrows,
    grecvedge,
    foldrecv,
    foldrecv2,
    onehot,
    onehot2,
    part,
    partrecv,
    gkrecv,
    total,
    totalrecv,
    full,
    final,
    sems,
):
    wch = WROWS // sectors
    kch = C // sectors
    chunk = wch + kch
    fch = final.shape[0] // sectors
    piece = totalrecv.shape[1]
    lat = lax.axis_index("lat")
    lon = lax.axis_index("lon")
    is_south = lat == 0
    is_north = lat == bands - 1

    def peer(dlat, dlon):
        return {
            "lat": lax.rem(lat + (dlat + bands), bands),
            "lon": lax.rem(lon + (dlon + sectors), sectors),
        }

    def send(src, dst, s, device):
        cp = pltpu.make_async_remote_copy(
            src_ref=src,
            dst_ref=dst,
            send_sem=sems.at[2 * s],
            recv_sem=sems.at[2 * s + 1],
            device_id=device,
            device_id_type=MESH,
        )
        cp.start()

    barrier = pltpu.get_barrier_semaphore()
    peers = [(o, 0) for o in range(1, bands)] + [(0, o) for o in range(1, sectors)]
    peers += [(1, 1), (1, -1), (-1, 1), (-1, -1)]
    for dlat, dlon in peers:
        pl.semaphore_signal(barrier, inc=1, device_id=peer(dlat, dlon), device_id_type=MESH)

    nat[...] = state[...].astype(F32)
    for j in range(TY):
        ext[3 + j] = nat[pl.ds(j, C, stride=TY), :]
    for k, j in enumerate((0, 1, 2, 5, 6, 7)):
        sendrows[k * C : (k + 1) * C, :] = ext[3 + j].astype(BF16)
    pack_edges(ext, packed)
    edge_messages(packed, sendedge.at[0], sendedge.at[1])

    seg = lax.broadcasted_iota(jnp.int32, (1, CELLS), 1)
    capacity = CELLS // bands
    filled = jnp.zeros((1, CELLS), jnp.int32)
    for p in range(bands):
        filled = jnp.where(seg // capacity == p, counts[0, p], filled)
    live = (seg % capacity) < filled
    row_of = jnp.right_shift(cells[...], 7)
    col_of = jnp.bitwise_and(cells[...], 127)
    in_row = (lax.broadcasted_iota(jnp.int32, (TY, CELLS), 0) == row_of) & live
    in_col = lax.broadcasted_iota(jnp.int32, (TX, CELLS), 0) == col_of
    wet[...] = dot_nt(
        jnp.where(in_row, 1.0, 0.0).astype(BF16), jnp.where(in_col, 1.0, 0.0).astype(BF16)
    )
    dkp = jnp.concatenate([dkt[...], jnp.zeros((128 - TAPS, C), F32)], axis=0).T
    for t in range(TAPS):
        kb[t] = jnp.broadcast_to(dkp[:, t : t + 1], (C, 128))

    pl.semaphore_wait(barrier, len(peers))

    def exchange(rows_s, edge_s, rows_r, edge_r, s):
        for n, dlat in enumerate((1, 0, -1)):
            send(edge_s.at[1], edge_r.at[n], s + 1, peer(dlat, 1))
            send(edge_s.at[0], edge_r.at[3 + n], s + 1, peer(dlat, -1))
        send(rows_s.at[pl.ds(0, 3 * C)], rows_r.at[pl.ds(3 * C, 3 * C)], s, peer(-1, 0))
        send(rows_s.at[pl.ds(3 * C, 3 * C)], rows_r.at[pl.ds(0, 3 * C)], s, peer(1, 0))

    exchange(sendrows, sendedge, recvrows, recvedge, 0)

    @pl.when(is_north)
    def _():
        for o in range(1, sectors):
            send(
                sendrows.at[pl.ds(3 * C, 3 * C)],
                foldrecv.at[pl.ds(lon * (3 * C), 3 * C)],
                2,
                peer(0, o),
            )

    gain_c = column(gain)
    scale_c = column(lscale)
    nat[...] = cot[...].astype(F32)
    for j in range(TY):
        x = nat[pl.ds(j, C, stride=TY), :]
        cotr[j] = x
        upstream[:, j * TX : (j + 1) * TX] = (wet[j : j + 1, :] * scale_c * x).astype(BF16)
    wexpt[...] = w_expand[...].astype(F32).T.astype(BF16)
    w_project[...] = wprojt[...].astype(F32).T.astype(BF16)

    left = lax.rem(lon + sectors - 1, sectors)
    right = lax.rem(lon + 1, sectors)

    @pl.when(is_north)
    def _():
        mine = partner[:, pl.ds(pl.multiple_of(lon * TX, TX), TX)]
        from_left = partner[:, pl.ds(pl.multiple_of(left * TX, TX), TX)]
        from_right = partner[:, pl.ds(pl.multiple_of(right * TX, TX), TX)]
        near = jnp.zeros((1, TX), jnp.int32)
        for r in range(3 + TY, EXT):
            near = jnp.where(slot_lanes((1, TX), 4 * r, 3), turn(from_left, 4 * r - 125), near)
            near = jnp.where(slot_lanes((1, TX), 64 + 4 * r, 3), turn(from_right, 64 + 4 * r), near)
        wanted = jnp.concatenate([mine, near], axis=1)
        for s in range(sectors):
            col = lax.broadcasted_iota(jnp.int32, (TX, 2 * TX), 0) + s * TX
            onehot[s] = jnp.where(col == wanted, 1.0, 0.0).astype(BF16)
        col = lax.broadcasted_iota(jnp.int32, (TX, sectors * TX), 0) + lon * TX
        for b in range(7):
            beside = partner[...] if b == 3 else pltpu.roll(partner[...], (3 - b) % (sectors * TX), 1)
            onehot2[b * TX : (b + 1) * TX, :] = jnp.where(beside == col, 1.0, 0.0).astype(BF16)
        foldrecv[pl.ds(lon * (3 * C), 3 * C), :] = sendrows[3 * C :, :]

    def each_tile(body, height):
        def step(ct, carry):
            body(pl.ds(pl.multiple_of(ct * height, 8), height))
            return carry

        lax.fori_loop(0, C // height, step, 0)

    def own_body(cs):
        acc = conv_own(ext, kb, cs, False, [jnp.zeros((cs.size, 128), F32) for _ in range(TY)])
        for j in range(TY):
            conv[j, cs, :] = acc[j]

    each_tile(own_body, 16)

    def fill_halo(rows_r, edge_r, rows, edges, s):
        wait_bytes(rows_r, sems.at[2 * s + 1])
        wait_bytes(edge_r, sems.at[2 * s + 3])
        for k in range(3):
            rows[k] = jnp.where(is_south, 0.0, rows_r[k * C : (k + 1) * C, :].astype(F32))
            rows[11 + k] = jnp.where(
                is_north, 0.0, rows_r[(3 + k) * C : (4 + k) * C, :].astype(F32)
            )
        unpack_edges(edge_r, edges, is_south, is_north)

    fill_halo(recvrows, recvedge, ext, edge, 0)

    def south_body(cs):
        acc = [conv[j, cs, :] for j in range(TY)]
        acc = conv_edge(edge, kb, cs, False, acc, 0)
        acc = conv_halo(ext, kb, cs, False, acc, True, False)
        for j in range(TY):
            conv[j, cs, :] = acc[j]

    each_tile(south_body, 24)

    def mlp_body(m, carry):
        at = pl.ds(pl.multiple_of(m * 256, 256), 256)
        v = jnp.concatenate([conv[2 * m], conv[2 * m + 1]], axis=1).astype(BF16).astype(F32)
        center = v - jnp.mean(v, axis=0, keepdims=True)
        variance = jnp.mean(center * center, axis=0, keepdims=True)
        inv_std = lax.rsqrt(variance + 1e-06)
        normed = center * inv_std
        sc = (normed * gain_c).astype(BF16)
        scaled[:, at] = sc
        up = upstream[:, at]
        for h in range(0, HID, 256):
            pre = dot_nn(wexpt[h : h + 256, :], sc)
            gh = dot_nn(w_project[h : h + 256, :], up)
            half = 0.5 * (1.0 + lax.erf(pre * ROOT_HALF))
            hidden[h : h + 256, at] = (pre * half).astype(BF16)
            slope = half + pre * jnp.exp(-0.5 * pre * pre) * ROOT_TWOPI_INV
            gradpre[h : h + 256, at] = (gh * slope).astype(BF16)
        branch = dot_nn(wprojt[...], hidden[:, at]).astype(BF16).astype(F32)
        gs = dot_nn(w_expand[...], gradpre[:, at]) * gain_c
        gr = inv_std * (
            gs
            - jnp.mean(gs, axis=0, keepdims=True)
            - normed * jnp.mean(gs * normed, axis=0, keepdims=True)
        )
        gr = gr.astype(BF16).astype(F32)
        for n in range(2):
            half_at = slice(n * TX, (n + 1) * TX)
            j = 2 * m + n
            b = wet[pl.ds(j, 1), :] * scale_c * branch[:, half_at]
            out_rows[j] = (ext[3 + j] + b).astype(BF16)
            gext[3 + j] = gr[:, half_at]
        return carry

    lax.fori_loop(0, TY // 4, mlp_body, 0)

    @pl.when(is_north)
    def _():
        wait_bytes(foldrecv.at[pl.ds(0, (sectors - 1) * 3 * C)], sems.at[5])
        corners = jnp.zeros((C, TX), F32)
        for k in range(3):
            acc = jnp.zeros((C, 2 * TX), F32)
            for s in range(sectors):
                base = s * 3 * C + (2 - k) * C
                acc = acc + dot_nn(foldrecv[base : base + C, :], onehot[s])
            ext[11 + k] = acc[:, :TX]
            at = 4 * (11 + k)
            here = slot_lanes((C, TX), at, 3) | slot_lanes((C, TX), 64 + at, 3)
            corners = jnp.where(here, acc[:, TX:], corners)
        fedge[...] = corners
        edge[...] = edge[...] + corners

        def corner_body(cs):
            acc = [None] * 5 + [conv[j, cs, :] for j in range(5, TY)]
            acc = conv_edge(fedge, kb, cs, False, acc, 5)
            for j in range(5, TY):
                conv[j, cs, :] = acc[j]

        each_tile(corner_body, 48)

    def north_body(cs):
        acc = [None] * 5 + [conv[j, cs, :] for j in range(5, TY)]
        acc = conv_halo(ext, kb, cs, False, acc, False, True)
        for j in range(5, TY):
            conv[j, cs, :] = acc[j]

    each_tile(north_body, 24)
    lax.fori_loop(TY // 4, TY // 2, mlp_body, 0)

    ge = dot_nt(scaled[...], gradpre[...]).astype(BF16)
    gpt = dot_nt(upstream[...], hidden[...]).astype(BF16)
    blocks = HID // 128
    for b in range(blocks):
        part[b * C : (b + 1) * C, :] = ge[:, b * 128 : (b + 1) * 128]
        part[(blocks + b) * C : (blocks + b + 1) * C, :] = gpt[:, b * 128 : (b + 1) * 128]
    for o in range(1, sectors):
        to = peer(0, o)
        send(part.at[pl.ds(to["lon"] * wch, wch)], partrecv.at[o - 1], 5, to)

    for k, j in enumerate((0, 1, 2, 5, 6, 7)):
        gsendrows[k * C : (k + 1) * C, :] = gext[3 + j].astype(BF16)
    pack_edges(gext, gpacked)
    edge_messages(gpacked, gsendedge.at[0], gsendedge.at[1])
    def gk_body(cs):
        lane = lax.broadcasted_iota(jnp.int32, (cs.size, 128), 1)
        x = ext[:, cs, :]
        g = gext[3 : 3 + TY, cs, :]
        terms = edge_terms(edge, cs)
        gp = gpacked[cs, :]
        beside = [turn(gp, 4 * a) for a in range(7)]
        res = jnp.zeros((cs.size, 128), F32)
        for d in range(7):
            y = shifted(g, 6 - d)
            for a in range(7):
                v = jnp.sum(x[a : a + TY] * y, axis=0)
                if d < 3:
                    v = v + jnp.where(lane < 64, terms[d] * beside[a], 0.0)
                if d > 3:
                    v = v + jnp.where(lane >= 64, terms[6 - d] * beside[a], 0.0)
                res = jnp.where(lane == 7 * a + d, jnp.sum(v, axis=1, keepdims=True), res)
        gk[cs, :] = res

    each_tile(gk_body, 16)
    for o in range(1, sectors):
        to = peer(0, o)
        send(gk.at[pl.ds(to["lon"] * kch, kch)], gkrecv.at[o - 1], 10, to)

    def adj_own_body(cs):
        acc = [cotr[j, cs, :] for j in range(TY)]
        acc = conv_own(gext, kb, cs, True, acc)
        for j in range(TY):
            conv[j, cs, :] = acc[j]

    each_tile(adj_own_body, 16)

    wait_bytes(partrecv, sems.at[11])
    own = part[pl.ds(pl.multiple_of(lon * wch, 16), wch), :].astype(F32)
    for o in range(1, sectors):
        own = own + partrecv[o - 1].astype(F32)
    total[0:wch, :] = own
    wait_bytes(gkrecv, sems.at[21])
    own = gk[pl.ds(pl.multiple_of(lon * kch, 8), kch), :]
    for o in range(1, sectors):
        own = own + gkrecv[o - 1]
    total[wch:chunk, :] = own
    if total.shape[0] > chunk:
        total[chunk:, :] = jnp.zeros((total.shape[0] - chunk, 128), F32)
    for o in range(1, bands):
        to = peer(o, 0)
        send(total.at[pl.ds(to["lat"] * piece, piece)], totalrecv.at[o - 1], 7, to)

    exchange(gsendrows, gsendedge, grecvrows, grecvedge, 3)

    @pl.when(is_north)
    def _():
        here = pl.ds(pl.multiple_of(lon * TX, TX), TX)
        for o in range(1, sectors):
            send(gsendrows.at[pl.ds(3 * C, 3 * C)], foldrecv2.at[:, here], 6, peer(0, o))
        foldrecv2[:, here] = gsendrows[3 * C :, :]

    mine = pl.ds(pl.multiple_of(lat * piece, 8), piece)
    acc = total[mine, :]
    wait_bytes(totalrecv, sems.at[15])
    for o in range(1, bands):
        acc = acc + totalrecv[o - 1]
    full[mine, :] = acc
    for o in range(1, bands):
        send(full.at[pl.ds(lat * piece, piece)], full.at[pl.ds(lat * piece, piece)], 8, peer(o, 0))
    fill_halo(grecvrows, grecvedge, gext, gedge, 3)

    def adj_halo_body(cs):
        acc = [conv[j, cs, :] for j in range(TY)]
        acc = conv_edge(gedge, kb, cs, True, acc, 0)
        acc = conv_halo(gext, kb, cs, True, acc, True, True)
        for j in range(TY):
            conv[j, cs, :] = acc[j]

    each_tile(adj_halo_body, 24)

    wait_bytes(full.at[pl.ds(0, (bands - 1) * piece)], sems.at[17])
    final[pl.ds(pl.multiple_of(lon * fch, 16), fch), :] = full[0:fch, :].astype(BF16)
    for o in range(1, sectors):
        send(final.at[pl.ds(lon * fch, fch)], final.at[pl.ds(lon * fch, fch)], 9, peer(0, o))

    @pl.when(is_north)
    def _():
        wait_bytes(foldrecv2.at[:, pl.ds(0, (sectors - 1) * TX)], sems.at[13])
        for r in range(3):
            near = dot_nt(foldrecv2[r * C : (r + 1) * C, :], onehot2[...])
            for k in range(r + 1):
                acc = conv[7 - k]
                for b in range(7):
                    acc = acc + kb[7 * (6 + k - r) + b] * near[:, b * TX : (b + 1) * TX]
                conv[7 - k] = acc

    for j in range(TY):
        grad_rows[j] = conv[j].astype(BF16)

    wait_bytes(final.at[pl.ds(0, (sectors - 1) * fch)], sems.at[19])
    sums_out[...] = final[...]

    wait_bytes(recvrows, sems.at[0])
    wait_bytes(recvedge, sems.at[2])
    wait_bytes(grecvrows, sems.at[6])
    wait_bytes(grecvedge, sems.at[8])
    wait_bytes(partrecv, sems.at[10])
    wait_bytes(gkrecv, sems.at[20])
    wait_bytes(totalrecv, sems.at[14])
    wait_bytes(totalrecv, sems.at[16])
    wait_bytes(final.at[pl.ds(0, (sectors - 1) * fch)], sems.at[18])

    @pl.when(is_north)
    def _():
        wait_bytes(foldrecv.at[pl.ds(0, (sectors - 1) * 3 * C)], sems.at[4])
        wait_bytes(foldrecv2.at[:, pl.ds(0, (sectors - 1) * TX)], sems.at[12])


def finish_kernel(
    sectors, out_rows, grad_rows, sums, out_field, grad_field, gkt, ge, gpt, nat
):
    wch = WROWS // sectors
    kch = C // sectors
    fch = sums.shape[0] // sectors
    for src, dst in ((out_rows, out_field), (grad_rows, grad_field)):
        for j in range(TY):
            nat[pl.ds(j, C, stride=TY), :] = src[j].astype(F32)
        dst[...] = nat[...].astype(BF16)
    blocks = HID // 128
    for b in range(2 * blocks):
        dst = ge if b < blocks else gpt
        lanes = slice((b % blocks) * 128, (b % blocks + 1) * 128)
        for r in range(0, C, PIECE):
            w = b * C + r
            at = (w // wch) * fch + w % wch
            dst[r : r + PIECE, lanes] = sums[at : at + PIECE, :].astype(F32)
    for n in range(sectors):
        at = n * fch + wch
        nat[n * kch : (n + 1) * kch, :] = sums[at : (n + 1) * fch, :].astype(F32)[:kch]
    gkt[...] = nat[0:C, :].T[:TAPS]


def on_device(
    bands,
    sectors,
    state_field,
    depth_kernel,
    norm_gain,
    w_expand,
    w_project,
    layer_scale,
    cotangent,
    send_cells,
    send_count,
    fold_partner,
):
    wch = WROWS // sectors
    kch = C // sectors
    fch = wch + -(-kch // 16) * 16
    piece = -(-fch // (8 * bands)) * 8
    vmem = pl.BlockSpec(memory_space=pltpu.VMEM)
    smem = pl.BlockSpec(memory_space=pltpu.SMEM)
    sds = jax.ShapeDtypeStruct
    rows3 = pltpu.VMEM((6 * C, 128), BF16)
    edge = pltpu.VMEM((6, GC, 128), BF16)
    fold = pltpu.VMEM((sectors * 3 * C, 128), BF16)
    scratch = dict(
        nat=pltpu.VMEM((C * TY, 128), F32),
        ext=pltpu.VMEM((EXT, C, 128), F32),
        gext=pltpu.VMEM((EXT, C, 128), F32),
        edge=pltpu.VMEM((C, 128), F32),
        gedge=pltpu.VMEM((C, 128), F32),
        packed=pltpu.VMEM((C, 128), F32),
        gpacked=pltpu.VMEM((C, 128), F32),
        cotr=pltpu.VMEM((TY, C, 128), F32),
        conv=pltpu.VMEM((TY, C, 128), F32),
        upstream=pltpu.VMEM((C, CELLS), BF16),
        scaled=pltpu.VMEM((C, CELLS), BF16),
        hidden=pltpu.VMEM((HID, CELLS), BF16),
        gradpre=pltpu.VMEM((HID, CELLS), BF16),
        wexpt=pltpu.VMEM((HID, C), BF16),
        w_project=pltpu.VMEM((HID, C), BF16),
        wet=pltpu.VMEM((TY, TX), F32),
        kb=pltpu.VMEM((TAPS, C, 128), F32),
        fedge=pltpu.VMEM((C, 128), F32),
        gk=pltpu.VMEM((C, 128), F32),
        sendrows=rows3,
        sendedge=pltpu.VMEM((2, GC, 128), BF16),
        recvrows=rows3,
        recvedge=edge,
        gsendrows=rows3,
        gsendedge=pltpu.VMEM((2, GC, 128), BF16),
        grecvrows=rows3,
        grecvedge=edge,
        foldrecv=fold,
        foldrecv2=pltpu.VMEM((3 * C, sectors * TX), BF16),
        onehot=pltpu.VMEM((sectors, TX, 2 * TX), BF16),
        onehot2=pltpu.VMEM((7 * TX, sectors * TX), BF16),
        part=pltpu.VMEM((WROWS, 128), BF16),
        partrecv=pltpu.VMEM((sectors - 1, wch, 128), BF16),
        gkrecv=pltpu.VMEM((sectors - 1, kch, 128), F32),
        total=pltpu.VMEM((bands * piece, 128), F32),
        totalrecv=pltpu.VMEM((bands - 1, piece, 128), F32),
        full=pltpu.VMEM((bands * piece, 128), F32),
        final=pltpu.VMEM((sectors * fch, 128), BF16),
        sems=pltpu.SemaphoreType.DMA((22,)),
    )
    out_rows, grad_rows, sums = pl.pallas_call(
        functools.partial(block_kernel, bands, sectors),
        out_shape=(
            sds((TY, C, 128), BF16),
            sds((TY, C, 128), BF16),
            sds((sectors * fch, 128), BF16),
        ),
        in_specs=[vmem] * 8 + [smem] + [vmem],
        out_specs=(vmem, vmem, vmem),
        scratch_shapes=list(scratch.values()),
        compiler_params=pltpu.CompilerParams(
            collective_id=0, has_side_effects=True, vmem_limit_bytes=48 * 2**20
        ),
        name="block",
    )(
        state_field.reshape(C * TY, TX),
        cotangent.reshape(C * TY, TX),
        depth_kernel.T,
        norm_gain.reshape(1, C),
        layer_scale.reshape(1, C),
        w_expand,
        w_project.T,
        send_cells,
        send_count,
        fold_partner.reshape(1, sectors * TX),
    )
    out_field, grad_field, gkt, ge, gpt = pl.pallas_call(
        functools.partial(finish_kernel, sectors),
        out_shape=(
            sds((C * TY, TX), BF16),
            sds((C * TY, TX), BF16),
            sds((TAPS, C), F32),
            sds((C, HID), F32),
            sds((C, HID), F32),
        ),
        in_specs=[vmem] * 3,
        out_specs=(vmem,) * 5,
        scratch_shapes=[pltpu.VMEM((C * TY, 128), F32)],
        compiler_params=pltpu.CompilerParams(vmem_limit_bytes=32 * 2**20),
        name="finish",
    )(out_rows, grad_rows, sums)
    return (
        out_field.reshape(C, TY, TX),
        grad_field.reshape(C, TY, TX),
        gkt.T,
        ge,
        gpt.T,
    )


def solution(mesh):
    return jax.shard_map(
        functools.partial(on_device, mesh.shape["lat"], mesh.shape["lon"]),
        mesh=mesh,
        in_specs=(
            P(None, "lat", "lon"),
            P(),
            P(),
            P(),
            P(),
            P(),
            P(None, "lat", "lon"),
            P("lat", "lon"),
            P("lat", "lon"),
            P(),
        ),
        out_specs=(P(None, "lat", "lon"), P(None, "lat", "lon"), P(), P(), P()),
        check_vma=False,
    )
```

```python
import functools

import jax
import jax.numpy as jnp
from jax import lax
from jax.experimental import pallas as pl
from jax.experimental.pallas import tpu as pltpu
from jax.sharding import PartitionSpec as P

MESH = pl.DeviceIdType.MESH
F32 = jnp.float32
BF16 = jnp.bfloat16
ROOT_HALF = 0.7071067811865476
ROOT_TWOPI_INV = 0.3989422804014327

C = 192
HID = 768
TY = 8
TX = 128
EXT = TY + 6
CELLS = TY * TX
TAPS = 49
GROUPS = 4
GC = C // GROUPS
WROWS = 2 * C * HID // 128
PIECE = 96


def dot_nn(a, b):
    return jnp.dot(a, b, preferred_element_type=F32)


def dot_nt(a, b):
    return lax.dot_general(a, b, (((1,), (1,)), ((), ())), preferred_element_type=F32)


def wait_bytes(ref, sem):
    pltpu.make_async_copy(ref, ref, sem).wait()


def column(row_ref):
    n = row_ref.shape[1]
    eye = lax.broadcasted_iota(jnp.int32, (n, n), 0) == lax.broadcasted_iota(
        jnp.int32, (n, n), 1
    )
    return jnp.sum(jnp.where(eye, row_ref[...], 0.0), axis=1, keepdims=True)


def slot_lanes(shape, base, n):
    lane = lax.broadcasted_iota(jnp.int32, shape, len(shape) - 1)
    return (lane >= base) & (lane < base + n)


def turn(x, shift):
    shift %= 128
    return pltpu.roll(x, shift, x.ndim - 1) if shift else x


def pack_edges(rows, packed):
    shape = (GC, 128)
    for q in range(GROUPS):
        at = slice(q * GC, (q + 1) * GC)
        p = jnp.zeros(shape, F32)
        for j in range(TY):
            x = rows[3 + j, at, :]
            p = jnp.where(slot_lanes(shape, 4 * j, 3), turn(x, 4 * j), p)
            p = jnp.where(slot_lanes(shape, 64 + 4 * j, 3), turn(x, 64 + 4 * j - 125), p)
        packed[at, :] = p


def edge_messages(packed, west, east):
    shape = (GC, 128)
    w = packed[0:GC, :]
    e = turn(w, 64)
    for q in range(1, GROUPS):
        x = packed[q * GC : (q + 1) * GC, :]
        here = slot_lanes(shape, 32 * q, 32)
        w = jnp.where(here, turn(x, 32 * q), w)
        e = jnp.where(here, turn(x, 32 * q - 64), e)
    west[...] = w.astype(BF16)
    east[...] = e.astype(BF16)


def unpack_edges(msgs, edge, is_south, is_north):
    shape = (GC, 128)
    lane = lax.broadcasted_iota(jnp.int32, shape, 1)
    within = jnp.bitwise_and(lane, 63)
    dead = (is_south & (within < 12)) | (is_north & (within >= 44))
    values = [msgs[n].astype(F32) for n in range(6)]
    for q in range(GROUPS):
        p = jnp.zeros(shape, F32)
        for side in range(2):
            for n, (at, width, j0) in enumerate(((0, 12, 5), (12, 32, 0), (44, 12, 0))):
                to = 64 * side + at
                x = turn(values[3 * side + n], to - 32 * q - 4 * j0)
                p = jnp.where(slot_lanes(shape, to, width), x, p)
        edge[q * GC : (q + 1) * GC, :] = jnp.where(dead, 0.0, p)


def shifted(x, d):
    sh = d - 3
    if sh == 0:
        return x
    lane = lax.broadcasted_iota(jnp.int32, x.shape, x.ndim - 1)
    x = jnp.where((lane >= sh) if sh > 0 else (lane < 128 + sh), x, 0.0)
    return turn(x, -sh)


def tap(a, d, reverse):
    t = 7 * a + d
    return TAPS - 1 - t if reverse else t


def conv_own(rows, kb, cs, reverse, acc):
    x = rows[3 : 3 + TY, cs, :]
    for d in range(7):
        y = shifted(x, d)
        for a in range(7):
            k = kb[tap(a, d, reverse), cs, :]
            for j in range(max(0, 3 - a), min(TY, 11 - a)):
                acc[j] = acc[j] + k * y[j + a - 3]
    return acc


def edge_terms(edge, cs):
    shape = (cs.size, 128)
    lane = lax.broadcasted_iota(jnp.int32, shape, 1)
    within = jnp.bitwise_and(lane, 3)
    left = lane < 64
    e = edge[cs, :]
    terms = [jnp.where(within < 3, e, 0.0)]
    for s in (1, 2):
        lf = jnp.where(left & (within <= 2 - s), turn(e, -s), 0.0)
        terms.append(
            jnp.where((lane >= 64) & (within >= s) & (within < 3), turn(e, s), lf)
        )
    return terms


def edge_sums(edge, kb, cs, reverse, depth):
    left = slot_lanes((cs.size, 128), 0, 64)
    terms = edge_terms(edge, cs)
    total = None
    for a in range(depth):
        y = None
        for s in range(3):
            lf = kb[tap(a, s, reverse), cs, :]
            rt = kb[tap(a, 6 - s, reverse), cs, :]
            k = jnp.where(left, lf, rt)
            y = k * terms[s] if y is None else y + k * terms[s]
        y = turn(y, -4 * a)
        total = y if total is None else total + y
    return total


def edge_row(total, j):
    west = jnp.where(slot_lanes(total.shape, 0, 3), turn(total, -4 * j), 0.0)
    return jnp.where(slot_lanes(total.shape, 125, 3), turn(total, 61 - 4 * j), west)


def conv_halo(rows, kb, cs, reverse, acc, south, north):
    if south:
        lo_rows = rows[0:3, cs, :]
    if north:
        hi_rows = rows[3 + TY :, cs, :]
    for d in range(7):
        if south:
            lo = shifted(lo_rows, d)
            for a in range(3):
                k = kb[tap(a, d, reverse), cs, :]
                for r in range(a, 3):
                    acc[r - a] = acc[r - a] + k * lo[r]
        if north:
            hi = shifted(hi_rows, d)
            for a in range(4, 7):
                k = kb[tap(a, d, reverse), cs, :]
                for r in range(0, a - 3):
                    acc[11 + r - a] = acc[11 + r - a] + k * hi[r]
    return acc


def conv_edge(edge, kb, cs, reverse, acc, first):
    total = edge_sums(edge, kb, cs, reverse, 7)
    for j in range(first, TY):
        acc[j] = acc[j] + edge_row(total, j)
    return acc


def block_kernel(
    bands,
    sectors,
    state_in,
    cot_in,
    dkt_in,
    gain_in,
    lscale_in,
    w_expand_in,
    wprojt_in,
    cells_in,
    counts,
    partner_in,
    out_nat,
    grad_nat,
    sums_out,
    nat,
    ext,
    gext,
    edge,
    gedge,
    packed,
    gpacked,
    cotr,
    conv,
    upstream,
    scaled,
    hidden,
    gradpre,
    wexpt,
    w_project,
    wet,
    kb,
    fedge,
    gk,
    sendrows,
    sendedge,
    recvrows,
    recvedge,
    gsendrows,
    gsendedge,
    grecvrows,
    grecvedge,
    foldrecv,
    foldrecv2,
    onehot,
    onehot2,
    part,
    partrecv,
    gkparts,
    gkrecv,
    gksum,
    gkall,
    total,
    totalrecv,
    full,
    final,
    sems,
    state,
    cot,
    dkt,
    gain,
    lscale,
    w_expand,
    wprojt,
    cells,
    partner,
    out_field,
    grad_field,
    loads,
):
    wch = WROWS // sectors
    kch = C // sectors
    fch = final.shape[0] // sectors
    piece = totalrecv.shape[1]
    lat = lax.axis_index("lat")
    lon = lax.axis_index("lon")
    is_south = lat == 0
    is_north = lat == bands - 1

    def peer(dlat, dlon):
        return {
            "lat": lax.rem(lat + (dlat + bands), bands),
            "lon": lax.rem(lon + (dlon + sectors), sectors),
        }

    def send(src, dst, s, device):
        cp = pltpu.make_async_remote_copy(
            src_ref=src,
            dst_ref=dst,
            send_sem=sems.at[2 * s],
            recv_sem=sems.at[2 * s + 1],
            device_id=device,
            device_id_type=MESH,
        )
        cp.start()

    sources = (
        (state_in, state),
        (dkt_in, dkt),
        (cot_in, cot),
        (w_expand_in, w_expand),
        (wprojt_in, wprojt),
        (gain_in, gain),
        (lscale_in, lscale),
        (cells_in, cells),
        (partner_in, partner),
    )
    copies = [
        pltpu.make_async_copy(src, dst, loads.at[n]) for n, (src, dst) in enumerate(sources)
    ]
    for cp in copies:
        cp.start()

    barrier = pltpu.get_barrier_semaphore()
    peers = [(o, 0) for o in range(1, bands)] + [(0, o) for o in range(1, sectors)]
    peers += [(1, 1), (1, -1), (-1, 1), (-1, -1)]
    for dlat, dlon in peers:
        pl.semaphore_signal(barrier, inc=1, device_id=peer(dlat, dlon), device_id_type=MESH)

    copies[0].wait()
    nat[...] = state[...].astype(F32)
    for j in range(TY):
        ext[3 + j] = nat[pl.ds(j, C, stride=TY), :]
    for k, j in enumerate((0, 1, 2, 5, 6, 7)):
        sendrows[k * C : (k + 1) * C, :] = ext[3 + j].astype(BF16)
    pack_edges(ext, packed)
    edge_messages(packed, sendedge.at[0], sendedge.at[1])

    pl.semaphore_wait(barrier, len(peers))

    def exchange(rows_s, edge_s, rows_r, edge_r, s):
        for n, dlat in enumerate((1, 0, -1)):
            send(edge_s.at[1], edge_r.at[n], s + 1, peer(dlat, 1))
            send(edge_s.at[0], edge_r.at[3 + n], s + 1, peer(dlat, -1))
        send(rows_s.at[pl.ds(0, 3 * C)], rows_r.at[pl.ds(3 * C, 3 * C)], s, peer(-1, 0))
        send(rows_s.at[pl.ds(3 * C, 3 * C)], rows_r.at[pl.ds(0, 3 * C)], s, peer(1, 0))

    exchange(sendrows, sendedge, recvrows, recvedge, 0)

    @pl.when(is_north)
    def _():
        for o in range(1, sectors):
            send(
                sendrows.at[pl.ds(3 * C, 3 * C)],
                foldrecv.at[pl.ds(lon * (3 * C), 3 * C)],
                2,
                peer(0, o),
            )

    for cp in copies[1:]:
        cp.wait()

    seg = lax.broadcasted_iota(jnp.int32, (1, CELLS), 1)
    capacity = CELLS // bands
    filled = jnp.zeros((1, CELLS), jnp.int32)
    for p in range(bands):
        filled = jnp.where(seg // capacity == p, counts[0, p], filled)
    live = (seg % capacity) < filled
    row_of = jnp.right_shift(cells[...], 7)
    col_of = jnp.bitwise_and(cells[...], 127)
    in_row = (lax.broadcasted_iota(jnp.int32, (TY, CELLS), 0) == row_of) & live
    in_col = lax.broadcasted_iota(jnp.int32, (TX, CELLS), 0) == col_of
    wet[...] = dot_nt(
        jnp.where(in_row, 1.0, 0.0).astype(BF16), jnp.where(in_col, 1.0, 0.0).astype(BF16)
    )
    dkp = jnp.concatenate([dkt[...], jnp.zeros((128 - TAPS, C), F32)], axis=0).T
    for t in range(TAPS):
        kb[t] = jnp.broadcast_to(dkp[:, t : t + 1], (C, 128))

    gain_c = column(gain)
    scale_c = column(lscale)
    nat[...] = cot[...].astype(F32)
    for j in range(TY):
        x = nat[pl.ds(j, C, stride=TY), :]
        cotr[j] = x
        upstream[:, j * TX : (j + 1) * TX] = (wet[j : j + 1, :] * scale_c * x).astype(BF16)
    wexpt[...] = w_expand[...].astype(F32).T.astype(BF16)
    w_project[...] = wprojt[...].astype(F32).T.astype(BF16)

    left = lax.rem(lon + sectors - 1, sectors)
    right = lax.rem(lon + 1, sectors)

    @pl.when(is_north)
    def _():
        mine = partner[:, pl.ds(pl.multiple_of(lon * TX, TX), TX)]
        from_left = partner[:, pl.ds(pl.multiple_of(left * TX, TX), TX)]
        from_right = partner[:, pl.ds(pl.multiple_of(right * TX, TX), TX)]
        near = jnp.zeros((1, TX), jnp.int32)
        for r in range(3 + TY, EXT):
            near = jnp.where(slot_lanes((1, TX), 4 * r, 3), turn(from_left, 4 * r - 125), near)
            near = jnp.where(slot_lanes((1, TX), 64 + 4 * r, 3), turn(from_right, 64 + 4 * r), near)
        wanted = jnp.concatenate([mine, near], axis=1)
        for s in range(sectors):
            col = lax.broadcasted_iota(jnp.int32, (TX, 2 * TX), 0) + s * TX
            onehot[s] = jnp.where(col == wanted, 1.0, 0.0).astype(BF16)
        col = lax.broadcasted_iota(jnp.int32, (TX, sectors * TX), 0) + lon * TX
        for b in range(7):
            beside = partner[...] if b == 3 else pltpu.roll(partner[...], (3 - b) % (sectors * TX), 1)
            onehot2[b * TX : (b + 1) * TX, :] = jnp.where(beside == col, 1.0, 0.0).astype(BF16)
        foldrecv[pl.ds(lon * (3 * C), 3 * C), :] = sendrows[3 * C :, :]

    def each_tile(body, height):
        def step(ct, carry):
            body(pl.ds(pl.multiple_of(ct * height, 8), height))
            return carry

        lax.fori_loop(0, C // height, step, 0)

    def own_body(cs):
        acc = conv_own(ext, kb, cs, False, [jnp.zeros((cs.size, 128), F32) for _ in range(TY)])
        for j in range(TY):
            conv[j, cs, :] = acc[j]

    each_tile(own_body, 16)

    def fill_halo(rows_r, edge_r, rows, edges, s):
        wait_bytes(rows_r, sems.at[2 * s + 1])
        wait_bytes(edge_r, sems.at[2 * s + 3])
        for k in range(3):
            rows[k] = jnp.where(is_south, 0.0, rows_r[k * C : (k + 1) * C, :].astype(F32))
            rows[11 + k] = jnp.where(
                is_north, 0.0, rows_r[(3 + k) * C : (4 + k) * C, :].astype(F32)
            )
        unpack_edges(edge_r, edges, is_south, is_north)

    fill_halo(recvrows, recvedge, ext, edge, 0)

    def south_body(cs):
        acc = [conv[j, cs, :] for j in range(TY)]
        acc = conv_edge(edge, kb, cs, False, acc, 0)
        acc = conv_halo(ext, kb, cs, False, acc, True, False)
        for j in range(TY):
            conv[j, cs, :] = acc[j]

    each_tile(south_body, 24)

    def mlp_body(m, carry):
        at = pl.ds(pl.multiple_of(m * 256, 256), 256)
        v = jnp.concatenate([conv[2 * m], conv[2 * m + 1]], axis=1).astype(BF16).astype(F32)
        center = v - jnp.mean(v, axis=0, keepdims=True)
        variance = jnp.mean(center * center, axis=0, keepdims=True)
        inv_std = lax.rsqrt(variance + 1e-06)
        normed = center * inv_std
        sc = (normed * gain_c).astype(BF16)
        scaled[:, at] = sc
        up = upstream[:, at]
        for h in range(0, HID, 256):
            pre = dot_nn(wexpt[h : h + 256, :], sc)
            gh = dot_nn(w_project[h : h + 256, :], up)
            half = 0.5 * (1.0 + lax.erf(pre * ROOT_HALF))
            hidden[h : h + 256, at] = (pre * half).astype(BF16)
            slope = half + pre * jnp.exp(-0.5 * pre * pre) * ROOT_TWOPI_INV
            gradpre[h : h + 256, at] = (gh * slope).astype(BF16)
        branch = dot_nn(wprojt[...], hidden[:, at]).astype(BF16).astype(F32)
        gs = dot_nn(w_expand[...], gradpre[:, at]) * gain_c
        gr = inv_std * (
            gs
            - jnp.mean(gs, axis=0, keepdims=True)
            - normed * jnp.mean(gs * normed, axis=0, keepdims=True)
        )
        gr = gr.astype(BF16).astype(F32)
        for n in range(2):
            half_at = slice(n * TX, (n + 1) * TX)
            j = 2 * m + n
            b = wet[pl.ds(j, 1), :] * scale_c * branch[:, half_at]
            nat[pl.ds(j, C, stride=TY), :] = ext[3 + j] + b
            gext[3 + j] = gr[:, half_at]
        return carry

    lax.fori_loop(0, TY // 4, mlp_body, 0)

    @pl.when(is_north)
    def _():
        wait_bytes(foldrecv.at[pl.ds(0, (sectors - 1) * 3 * C)], sems.at[5])
        corners = jnp.zeros((C, TX), F32)
        for k in range(3):
            acc = jnp.zeros((C, 2 * TX), F32)
            for s in range(sectors):
                base = s * 3 * C + (2 - k) * C
                acc = acc + dot_nn(foldrecv[base : base + C, :], onehot[s])
            ext[11 + k] = acc[:, :TX]
            at = 4 * (11 + k)
            here = slot_lanes((C, TX), at, 3) | slot_lanes((C, TX), 64 + at, 3)
            corners = jnp.where(here, acc[:, TX:], corners)
        fedge[...] = corners
        edge[...] = edge[...] + corners

        def corner_body(cs):
            acc = [None] * 5 + [conv[j, cs, :] for j in range(5, TY)]
            acc = conv_edge(fedge, kb, cs, False, acc, 5)
            for j in range(5, TY):
                conv[j, cs, :] = acc[j]

        each_tile(corner_body, 48)

    def north_body(cs):
        acc = [None] * 5 + [conv[j, cs, :] for j in range(5, TY)]
        acc = conv_halo(ext, kb, cs, False, acc, False, True)
        for j in range(5, TY):
            conv[j, cs, :] = acc[j]

    each_tile(north_body, 24)
    lax.fori_loop(TY // 4, TY // 2, mlp_body, 0)

    ge = dot_nt(scaled[...], gradpre[...]).astype(BF16)
    gpt = dot_nt(upstream[...], hidden[...]).astype(BF16)
    blocks = HID // 128
    for b in range(blocks):
        part[b * C : (b + 1) * C, :] = ge[:, b * 128 : (b + 1) * 128]
        part[(blocks + b) * C : (blocks + b + 1) * C, :] = gpt[:, b * 128 : (b + 1) * 128]
    for o in range(1, sectors):
        to = peer(0, o)
        send(part.at[pl.ds(to["lon"] * wch, wch)], partrecv.at[o - 1], 5, to)

    out_field[...] = nat[...].astype(BF16)
    out_copy = pltpu.make_async_copy(out_field, out_nat, loads.at[0])
    out_copy.start()

    for k, j in enumerate((0, 1, 2, 5, 6, 7)):
        gsendrows[k * C : (k + 1) * C, :] = gext[3 + j].astype(BF16)
    pack_edges(gext, gpacked)
    edge_messages(gpacked, gsendedge.at[0], gsendedge.at[1])
    def gk_body(cs):
        lane = lax.broadcasted_iota(jnp.int32, (cs.size, 128), 1)
        x = ext[:, cs, :]
        g = gext[3 : 3 + TY, cs, :]
        terms = edge_terms(edge, cs)
        gp = gpacked[cs, :]
        beside = [turn(gp, 4 * a) for a in range(7)]
        for d in range(7):
            y = shifted(g, 6 - d)
            for a in range(7):
                v = jnp.sum(x[a : a + TY] * y, axis=0)
                if d < 3:
                    v = v + jnp.where(lane < 64, terms[d] * beside[a], 0.0)
                if d > 3:
                    v = v + jnp.where(lane >= 64, terms[6 - d] * beside[a], 0.0)
                gkparts[7 * a + d, cs, :] = v

    each_tile(gk_body, 8)
    lane = lax.broadcasted_iota(jnp.int32, (C, 128), 1)
    ones = jnp.ones((128, 128), BF16)
    res = jnp.zeros((C, 128), F32)
    for a in range(7):
        v = gkparts[7 * a : 7 * a + 7].reshape(7 * C, 128)
        hi = v.astype(BF16)
        lo = (v - hi.astype(F32)).astype(BF16)
        v = dot_nn(hi, ones) + dot_nn(lo, ones)
        for d in range(7):
            res = jnp.where(lane == 7 * a + d, v[d * C : (d + 1) * C], res)
    gk[...] = res
    for o in range(1, sectors):
        to = peer(0, o)
        send(gk.at[pl.ds(to["lon"] * kch, kch)], gkrecv.at[o - 1], 10, to)

    wait_bytes(partrecv, sems.at[11])
    own = part[pl.ds(pl.multiple_of(lon * wch, 16), wch), :].astype(F32)
    for o in range(1, sectors):
        own = own + partrecv[o - 1].astype(F32)
    total[0:wch, :] = own
    if total.shape[0] > wch:
        total[wch:, :] = jnp.zeros((total.shape[0] - wch, 128), F32)
    for o in range(1, bands):
        to = peer(o, 0)
        send(total.at[pl.ds(to["lat"] * piece, piece)], totalrecv.at[o - 1], 7, to)

    exchange(gsendrows, gsendedge, grecvrows, grecvedge, 3)

    @pl.when(is_north)
    def _():
        here = pl.ds(pl.multiple_of(lon * TX, TX), TX)
        for o in range(1, sectors):
            send(gsendrows.at[pl.ds(3 * C, 3 * C)], foldrecv2.at[:, here], 6, peer(0, o))
        foldrecv2[:, here] = gsendrows[3 * C :, :]

    wait_bytes(gkrecv, sems.at[21])
    own = gk[pl.ds(pl.multiple_of(lon * kch, 8), kch), :]
    for o in range(1, sectors):
        own = own + gkrecv[o - 1]
    gksum[...] = own
    for o in range(1, bands):
        send(gksum, gkall.at[o - 1], 11, peer(o, 0))

    mine = pl.ds(pl.multiple_of(lat * piece, 8), piece)
    acc = total[mine, :]
    wait_bytes(totalrecv, sems.at[15])
    for o in range(1, bands):
        acc = acc + totalrecv[o - 1]
    full[mine, :] = acc
    for o in range(1, bands):
        send(full.at[pl.ds(lat * piece, piece)], full.at[pl.ds(lat * piece, piece)], 8, peer(o, 0))
    def adj_own_body(cs):
        acc = [cotr[j, cs, :] for j in range(TY)]
        acc = conv_own(gext, kb, cs, True, acc)
        for j in range(TY):
            conv[j, cs, :] = acc[j]

    each_tile(adj_own_body, 16)

    wait_bytes(full.at[pl.ds(0, (bands - 1) * piece)], sems.at[17])
    base = pl.multiple_of(lon * fch, 16)
    final[pl.ds(base, wch), :] = full[0:wch, :].astype(BF16)
    wait_bytes(gkall, sems.at[23])
    own = gksum[...]
    for o in range(1, bands):
        own = own + gkall[o - 1]
    tail = jnp.zeros((fch - wch - kch, 128), F32)
    final[pl.ds(base + wch, fch - wch), :] = jnp.concatenate([own, tail], axis=0).astype(BF16)
    for o in range(1, sectors):
        send(final.at[pl.ds(lon * fch, fch)], final.at[pl.ds(lon * fch, fch)], 9, peer(0, o))

    fill_halo(grecvrows, grecvedge, gext, gedge, 3)

    def adj_halo_body(cs):
        acc = [conv[j, cs, :] for j in range(TY)]
        acc = conv_edge(gedge, kb, cs, True, acc, 0)
        acc = conv_halo(gext, kb, cs, True, acc, True, True)
        for j in range(TY):
            conv[j, cs, :] = acc[j]

    each_tile(adj_halo_body, 24)

    @pl.when(is_north)
    def _():
        wait_bytes(foldrecv2.at[:, pl.ds(0, (sectors - 1) * TX)], sems.at[13])
        for r in range(3):
            near = dot_nt(foldrecv2[r * C : (r + 1) * C, :], onehot2[...])
            for k in range(r + 1):
                acc = conv[7 - k]
                for b in range(7):
                    acc = acc + kb[7 * (6 + k - r) + b] * near[:, b * TX : (b + 1) * TX]
                conv[7 - k] = acc

    for j in range(TY):
        nat[pl.ds(j, C, stride=TY), :] = conv[j]
    grad_field[...] = nat[...].astype(BF16)
    grad_copy = pltpu.make_async_copy(grad_field, grad_nat, loads.at[1])
    grad_copy.start()

    wait_bytes(final.at[pl.ds(0, (sectors - 1) * fch)], sems.at[19])
    sums_copy = pltpu.make_async_copy(final, sums_out, loads.at[2])
    sums_copy.start()

    out_copy.wait()
    grad_copy.wait()
    sums_copy.wait()
    wait_bytes(recvrows, sems.at[0])
    wait_bytes(recvedge, sems.at[2])
    wait_bytes(grecvrows, sems.at[6])
    wait_bytes(grecvedge, sems.at[8])
    wait_bytes(partrecv, sems.at[10])
    wait_bytes(gkrecv, sems.at[20])
    wait_bytes(gkall, sems.at[22])
    wait_bytes(totalrecv, sems.at[14])
    wait_bytes(totalrecv, sems.at[16])
    wait_bytes(final.at[pl.ds(0, (sectors - 1) * fch)], sems.at[18])

    @pl.when(is_north)
    def _():
        wait_bytes(foldrecv.at[pl.ds(0, (sectors - 1) * 3 * C)], sems.at[4])
        wait_bytes(foldrecv2.at[:, pl.ds(0, (sectors - 1) * TX)], sems.at[12])


def finish_kernel(
    sectors,
    out_nat,
    grad_nat,
    sums_in,
    out_field,
    grad_field,
    gkt,
    ge_out,
    gpt_out,
    gk,
    sums,
    fields,
    ge,
    gpt,
    sems,
):
    wch = WROWS // sectors
    kch = C // sectors
    fch = sums.shape[0] // sectors
    load = pltpu.make_async_copy(sums_in, sums, sems.at[2])
    load.start()
    loads = [
        pltpu.make_async_copy(src, fields.at[n], sems.at[n])
        for n, src in enumerate((out_nat, grad_nat))
    ]
    for cp in loads:
        cp.start()
    load.wait()
    stores = []
    blocks = HID // 128
    for n, (dst, out) in enumerate(((ge, ge_out), (gpt, gpt_out))):
        for b in range(blocks):
            lanes = slice(b * 128, (b + 1) * 128)
            for r in range(0, C, PIECE):
                w = (n * blocks + b) * C + r
                at = (w // wch) * fch + w % wch
                dst[r : r + PIECE, lanes] = sums[at : at + PIECE, :].astype(F32)
        stores.append(pltpu.make_async_copy(dst, out, sems.at[3 + n]))
        stores[-1].start()
    for n, (cp, dst) in enumerate(zip(loads, (out_field, grad_field))):
        cp.wait()
        stores.append(pltpu.make_async_copy(fields.at[n], dst, sems.at[5 + n]))
        stores[-1].start()
    for n in range(sectors):
        at = n * fch + wch
        gk[n * kch : (n + 1) * kch, :] = sums[at : (n + 1) * fch, :].astype(F32)[:kch]
    gkt[...] = gk[...].T[:TAPS]
    for cp in stores:
        cp.wait()


def on_device(
    bands,
    sectors,
    state_field,
    depth_kernel,
    norm_gain,
    w_expand,
    w_project,
    layer_scale,
    cotangent,
    send_cells,
    send_count,
    fold_partner,
):
    wch = WROWS // sectors
    kch = C // sectors
    fch = wch + -(-kch // 16) * 16
    piece = -(-wch // (8 * bands)) * 8
    vmem = pl.BlockSpec(memory_space=pltpu.VMEM)
    hbm = pl.BlockSpec(memory_space=pltpu.HBM)
    smem = pl.BlockSpec(memory_space=pltpu.SMEM)
    sds = jax.ShapeDtypeStruct
    rows3 = pltpu.VMEM((6 * C, 128), BF16)
    edge = pltpu.VMEM((6, GC, 128), BF16)
    fold = pltpu.VMEM((sectors * 3 * C, 128), BF16)
    scratch = dict(
        nat=pltpu.VMEM((C * TY, 128), F32),
        ext=pltpu.VMEM((EXT, C, 128), F32),
        gext=pltpu.VMEM((EXT, C, 128), F32),
        edge=pltpu.VMEM((C, 128), F32),
        gedge=pltpu.VMEM((C, 128), F32),
        packed=pltpu.VMEM((C, 128), F32),
        gpacked=pltpu.VMEM((C, 128), F32),
        cotr=pltpu.VMEM((TY, C, 128), F32),
        conv=pltpu.VMEM((TY, C, 128), F32),
        upstream=pltpu.VMEM((C, CELLS), BF16),
        scaled=pltpu.VMEM((C, CELLS), BF16),
        hidden=pltpu.VMEM((HID, CELLS), BF16),
        gradpre=pltpu.VMEM((HID, CELLS), BF16),
        wexpt=pltpu.VMEM((HID, C), BF16),
        w_project=pltpu.VMEM((HID, C), BF16),
        wet=pltpu.VMEM((TY, TX), F32),
        kb=pltpu.VMEM((TAPS, C, 128), F32),
        fedge=pltpu.VMEM((C, 128), F32),
        gk=pltpu.VMEM((C, 128), F32),
        sendrows=rows3,
        sendedge=pltpu.VMEM((2, GC, 128), BF16),
        recvrows=rows3,
        recvedge=edge,
        gsendrows=rows3,
        gsendedge=pltpu.VMEM((2, GC, 128), BF16),
        grecvrows=rows3,
        grecvedge=edge,
        foldrecv=fold,
        foldrecv2=pltpu.VMEM((3 * C, sectors * TX), BF16),
        onehot=pltpu.VMEM((sectors, TX, 2 * TX), BF16),
        onehot2=pltpu.VMEM((7 * TX, sectors * TX), BF16),
        part=pltpu.VMEM((WROWS, 128), BF16),
        partrecv=pltpu.VMEM((sectors - 1, wch, 128), BF16),
        gkparts=pltpu.VMEM((TAPS, C, 128), F32),
        gkrecv=pltpu.VMEM((sectors - 1, kch, 128), F32),
        gksum=pltpu.VMEM((kch, 128), F32),
        gkall=pltpu.VMEM((bands - 1, kch, 128), F32),
        total=pltpu.VMEM((bands * piece, 128), F32),
        totalrecv=pltpu.VMEM((bands - 1, piece, 128), F32),
        full=pltpu.VMEM((bands * piece, 128), F32),
        final=pltpu.VMEM((sectors * fch, 128), BF16),
        sems=pltpu.SemaphoreType.DMA((24,)),
        state=pltpu.VMEM((C * TY, TX), BF16),
        cot=pltpu.VMEM((C * TY, TX), BF16),
        dkt=pltpu.VMEM((TAPS, C), F32),
        gain=pltpu.VMEM((1, C), F32),
        lscale=pltpu.VMEM((1, C), F32),
        w_expand=pltpu.VMEM((C, HID), BF16),
        wprojt=pltpu.VMEM((C, HID), BF16),
        cells=pltpu.VMEM((1, CELLS), jnp.int32),
        partner=pltpu.VMEM((1, sectors * TX), jnp.int32),
        out_field=pltpu.VMEM((C * TY, TX), BF16),
        grad_field=pltpu.VMEM((C * TY, TX), BF16),
        loads=pltpu.SemaphoreType.DMA((9,)),
    )
    out_nat, grad_nat, sums = pl.pallas_call(
        functools.partial(block_kernel, bands, sectors),
        out_shape=(
            sds((C * TY, TX), BF16),
            sds((C * TY, TX), BF16),
            sds((sectors * fch, 128), BF16),
        ),
        in_specs=[hbm] * 8 + [smem] + [hbm],
        out_specs=(hbm, hbm, hbm),
        scratch_shapes=list(scratch.values()),
        compiler_params=pltpu.CompilerParams(
            collective_id=0, has_side_effects=True, vmem_limit_bytes=60 * 2**20
        ),
        name="block",
    )(
        state_field.reshape(C * TY, TX),
        cotangent.reshape(C * TY, TX),
        depth_kernel.T,
        norm_gain.reshape(1, C),
        layer_scale.reshape(1, C),
        w_expand,
        w_project.T,
        send_cells,
        send_count,
        fold_partner.reshape(1, sectors * TX),
    )
    out_field, grad_field, gkt, ge, gpt = pl.pallas_call(
        functools.partial(finish_kernel, sectors),
        out_shape=(
            sds((C * TY, TX), BF16),
            sds((C * TY, TX), BF16),
            sds((TAPS, C), F32),
            sds((C, HID), F32),
            sds((C, HID), F32),
        ),
        in_specs=[hbm, hbm, hbm],
        out_specs=(hbm, hbm, vmem, hbm, hbm),
        scratch_shapes=[
            pltpu.VMEM((C, 128), F32),
            pltpu.VMEM((sectors * fch, 128), BF16),
            pltpu.VMEM((2, C * TY, TX), BF16),
            pltpu.VMEM((C, HID), F32),
            pltpu.VMEM((C, HID), F32),
            pltpu.SemaphoreType.DMA((7,)),
        ],
        compiler_params=pltpu.CompilerParams(vmem_limit_bytes=60 * 2**20),
        name="finish",
    )(out_nat, grad_nat, sums)
    return (
        out_field.reshape(C, TY, TX),
        grad_field.reshape(C, TY, TX),
        gkt.T,
        ge,
        gpt.T,
    )


def solution(mesh):
    return jax.shard_map(
        functools.partial(on_device, mesh.shape["lat"], mesh.shape["lon"]),
        mesh=mesh,
        in_specs=(
            P(None, "lat", "lon"),
            P(),
            P(),
            P(),
            P(),
            P(),
            P(None, "lat", "lon"),
            P("lat", "lon"),
            P("lat", "lon"),
            P(),
        ),
        out_specs=(P(None, "lat", "lon"), P(None, "lat", "lon"), P(), P(), P()),
        check_vma=False,
    )
```

```python
import functools

import jax
import jax.numpy as jnp
from jax import lax
from jax.experimental import pallas as pl
from jax.experimental.pallas import tpu as pltpu
from jax.sharding import PartitionSpec as P

MESH = pl.DeviceIdType.MESH
F32 = jnp.float32
BF16 = jnp.bfloat16
ROOT_HALF = 0.7071067811865476
ROOT_TWOPI_INV = 0.3989422804014327

C = 192
HID = 768
TY = 8
TX = 128
EXT = TY + 6
CELLS = TY * TX
TAPS = 49
GROUPS = 4
GC = C // GROUPS
WROWS = 2 * C * HID // 128
PIECE = 48


def dot_nn(a, b):
    return jnp.dot(a, b, preferred_element_type=F32)


def dot_nt(a, b):
    return lax.dot_general(a, b, (((1,), (1,)), ((), ())), preferred_element_type=F32)


def wait_bytes(ref, sem):
    pltpu.make_async_copy(ref, ref, sem).wait()


def column(row_ref):
    n = row_ref.shape[1]
    eye = lax.broadcasted_iota(jnp.int32, (n, n), 0) == lax.broadcasted_iota(
        jnp.int32, (n, n), 1
    )
    return jnp.sum(jnp.where(eye, row_ref[...], 0.0), axis=1, keepdims=True)


def slot_lanes(shape, base, n):
    lane = lax.broadcasted_iota(jnp.int32, shape, len(shape) - 1)
    return (lane >= base) & (lane < base + n)


def turn(x, shift):
    shift %= 128
    return pltpu.roll(x, shift, x.ndim - 1) if shift else x


def pack_edges(rows, packed):
    shape = (GC, 128)
    for q in range(GROUPS):
        at = slice(q * GC, (q + 1) * GC)
        p = jnp.zeros(shape, F32)
        for j in range(TY):
            x = rows[3 + j, at, :]
            p = jnp.where(slot_lanes(shape, 4 * j, 3), turn(x, 4 * j), p)
            p = jnp.where(slot_lanes(shape, 64 + 4 * j, 3), turn(x, 64 + 4 * j - 125), p)
        packed[at, :] = p


def edge_messages(packed, west, east):
    shape = (GC, 128)
    w = packed[0:GC, :]
    e = turn(w, 64)
    for q in range(1, GROUPS):
        x = packed[q * GC : (q + 1) * GC, :]
        here = slot_lanes(shape, 32 * q, 32)
        w = jnp.where(here, turn(x, 32 * q), w)
        e = jnp.where(here, turn(x, 32 * q - 64), e)
    west[...] = w.astype(BF16)
    east[...] = e.astype(BF16)


def unpack_edges(msgs, edge, is_south, is_north):
    shape = (GC, 128)
    lane = lax.broadcasted_iota(jnp.int32, shape, 1)
    within = jnp.bitwise_and(lane, 63)
    dead = (is_south & (within < 12)) | (is_north & (within >= 44))
    values = [msgs[n].astype(F32) for n in range(6)]
    for q in range(GROUPS):
        p = jnp.zeros(shape, F32)
        for side in range(2):
            for n, (at, width, j0) in enumerate(((0, 12, 5), (12, 32, 0), (44, 12, 0))):
                to = 64 * side + at
                x = turn(values[3 * side + n], to - 32 * q - 4 * j0)
                p = jnp.where(slot_lanes(shape, to, width), x, p)
        edge[q * GC : (q + 1) * GC, :] = jnp.where(dead, 0.0, p)


def shifted(x, d):
    sh = d - 3
    if sh == 0:
        return x
    lane = lax.broadcasted_iota(jnp.int32, x.shape, x.ndim - 1)
    x = jnp.where((lane >= sh) if sh > 0 else (lane < 128 + sh), x, 0.0)
    return turn(x, -sh)


def tap(a, d, reverse):
    t = 7 * a + d
    return TAPS - 1 - t if reverse else t


def conv_own(rows, kb, cs, reverse, acc):
    x = rows[3 : 3 + TY, cs, :]
    for d in range(7):
        y = shifted(x, d)
        for a in range(7):
            k = kb[tap(a, d, reverse), cs, :]
            for j in range(max(0, 3 - a), min(TY, 11 - a)):
                acc[j] = acc[j] + k * y[j + a - 3]
    return acc


def edge_terms(edge, cs):
    shape = (cs.size, 128)
    lane = lax.broadcasted_iota(jnp.int32, shape, 1)
    within = jnp.bitwise_and(lane, 3)
    left = lane < 64
    e = edge[cs, :]
    terms = [jnp.where(within < 3, e, 0.0)]
    for s in (1, 2):
        lf = jnp.where(left & (within <= 2 - s), turn(e, -s), 0.0)
        terms.append(
            jnp.where((lane >= 64) & (within >= s) & (within < 3), turn(e, s), lf)
        )
    return terms


def edge_sums(edge, kb, cs, reverse, depth):
    left = slot_lanes((cs.size, 128), 0, 64)
    terms = edge_terms(edge, cs)
    total = None
    for a in range(depth):
        y = None
        for s in range(3):
            lf = kb[tap(a, s, reverse), cs, :]
            rt = kb[tap(a, 6 - s, reverse), cs, :]
            k = jnp.where(left, lf, rt)
            y = k * terms[s] if y is None else y + k * terms[s]
        y = turn(y, -4 * a)
        total = y if total is None else total + y
    return total


def edge_row(total, j):
    west = jnp.where(slot_lanes(total.shape, 0, 3), turn(total, -4 * j), 0.0)
    return jnp.where(slot_lanes(total.shape, 125, 3), turn(total, 61 - 4 * j), west)


def conv_halo(rows, kb, cs, reverse, acc, south, north):
    if south:
        lo_rows = rows[0:3, cs, :]
    if north:
        hi_rows = rows[3 + TY :, cs, :]
    for d in range(7):
        if south:
            lo = shifted(lo_rows, d)
            for a in range(3):
                k = kb[tap(a, d, reverse), cs, :]
                for r in range(a, 3):
                    acc[r - a] = acc[r - a] + k * lo[r]
        if north:
            hi = shifted(hi_rows, d)
            for a in range(4, 7):
                k = kb[tap(a, d, reverse), cs, :]
                for r in range(0, a - 3):
                    acc[11 + r - a] = acc[11 + r - a] + k * hi[r]
    return acc


def conv_edge(edge, kb, cs, reverse, acc, first):
    total = edge_sums(edge, kb, cs, reverse, 7)
    for j in range(first, TY):
        acc[j] = acc[j] + edge_row(total, j)
    return acc


def block_kernel(
    bands,
    sectors,
    state_in,
    cot_in,
    dkt_in,
    gain_in,
    lscale_in,
    w_expand_in,
    wprojt_in,
    cells_in,
    counts,
    partner_in,
    out_nat,
    grad_nat,
    sums_out,
    nat,
    ext,
    gext,
    edge,
    gedge,
    packed,
    gpacked,
    cotr,
    conv,
    upstream,
    scaled,
    hidden,
    gradpre,
    wexpt,
    w_project,
    wet,
    kb,
    fedge,
    gk,
    sendrows,
    sendedge,
    recvrows,
    recvedge,
    gsendrows,
    gsendedge,
    grecvrows,
    grecvedge,
    foldrecv,
    foldrecv2,
    onehot,
    onehot2,
    part,
    besiderecv,
    halfsum,
    partrecv,
    gkparts,
    gkrecv,
    gksum,
    gkall,
    total,
    totalrecv,
    full,
    final,
    sems,
    state,
    cot,
    dkt,
    gain,
    lscale,
    w_expand,
    wprojt,
    cells,
    partner,
    out_field,
    grad_field,
    loads,
):
    half_rows = WROWS // 2
    wch = half_rows // sectors
    kch = C // sectors
    fch = final.shape[0] // (2 * sectors)
    chips = bands // 2
    piece = totalrecv.shape[1]
    lat = lax.axis_index("lat")
    lon = lax.axis_index("lon")
    core = lax.rem(lat, 2)
    chip = lat // 2
    is_south = lat == 0
    is_north = lat == bands - 1

    def peer(dlat, dlon):
        return {
            "lat": lax.rem(lat + (dlat + bands), bands),
            "lon": lax.rem(lon + (dlon + sectors), sectors),
        }

    beside = {"lat": lat + 1 - 2 * core, "lon": lon}

    def send(src, dst, s, device):
        cp = pltpu.make_async_remote_copy(
            src_ref=src,
            dst_ref=dst,
            send_sem=sems.at[2 * s],
            recv_sem=sems.at[2 * s + 1],
            device_id=device,
            device_id_type=MESH,
        )
        cp.start()

    sources = (
        (state_in, state),
        (dkt_in, dkt),
        (cot_in, cot),
        (w_expand_in, w_expand),
        (wprojt_in, wprojt),
        (gain_in, gain),
        (lscale_in, lscale),
        (cells_in, cells),
        (partner_in, partner),
    )
    copies = [
        pltpu.make_async_copy(src, dst, loads.at[n]) for n, (src, dst) in enumerate(sources)
    ]
    for cp in copies:
        cp.start()

    barrier = pltpu.get_barrier_semaphore()
    peers = [(o, 0) for o in range(1, bands)] + [(0, o) for o in range(1, sectors)]
    peers += [(1, 1), (1, -1), (-1, 1), (-1, -1)]
    for dlat, dlon in peers:
        pl.semaphore_signal(barrier, inc=1, device_id=peer(dlat, dlon), device_id_type=MESH)

    copies[0].wait()
    nat[...] = state[...].astype(F32)
    for j in range(TY):
        ext[3 + j] = nat[pl.ds(j, C, stride=TY), :]
    for k, j in enumerate((0, 1, 2, 5, 6, 7)):
        sendrows[k * C : (k + 1) * C, :] = ext[3 + j].astype(BF16)
    pack_edges(ext, packed)
    edge_messages(packed, sendedge.at[0], sendedge.at[1])

    pl.semaphore_wait(barrier, len(peers))

    def exchange(rows_s, edge_s, rows_r, edge_r, s):
        for n, dlat in enumerate((1, 0, -1)):
            send(edge_s.at[1], edge_r.at[n], s + 1, peer(dlat, 1))
            send(edge_s.at[0], edge_r.at[3 + n], s + 1, peer(dlat, -1))
        send(rows_s.at[pl.ds(0, 3 * C)], rows_r.at[pl.ds(3 * C, 3 * C)], s, peer(-1, 0))
        send(rows_s.at[pl.ds(3 * C, 3 * C)], rows_r.at[pl.ds(0, 3 * C)], s, peer(1, 0))

    exchange(sendrows, sendedge, recvrows, recvedge, 0)

    @pl.when(is_north)
    def _():
        for o in range(1, sectors):
            send(
                sendrows.at[pl.ds(3 * C, 3 * C)],
                foldrecv.at[pl.ds(lon * (3 * C), 3 * C)],
                2,
                peer(0, o),
            )

    for cp in copies[1:]:
        cp.wait()

    seg = lax.broadcasted_iota(jnp.int32, (1, CELLS), 1)
    capacity = CELLS // bands
    filled = jnp.zeros((1, CELLS), jnp.int32)
    for p in range(bands):
        filled = jnp.where(seg // capacity == p, counts[0, p], filled)
    live = (seg % capacity) < filled
    row_of = jnp.right_shift(cells[...], 7)
    col_of = jnp.bitwise_and(cells[...], 127)
    in_row = (lax.broadcasted_iota(jnp.int32, (TY, CELLS), 0) == row_of) & live
    in_col = lax.broadcasted_iota(jnp.int32, (TX, CELLS), 0) == col_of
    wet[...] = dot_nt(
        jnp.where(in_row, 1.0, 0.0).astype(BF16), jnp.where(in_col, 1.0, 0.0).astype(BF16)
    )
    dkp = jnp.concatenate([dkt[...], jnp.zeros((128 - TAPS, C), F32)], axis=0).T
    for t in range(TAPS):
        kb[t] = jnp.broadcast_to(dkp[:, t : t + 1], (C, 128))

    gain_c = column(gain)
    scale_c = column(lscale)
    nat[...] = cot[...].astype(F32)
    for j in range(TY):
        x = nat[pl.ds(j, C, stride=TY), :]
        cotr[j] = x
        upstream[:, j * TX : (j + 1) * TX] = (wet[j : j + 1, :] * scale_c * x).astype(BF16)
    wexpt[...] = w_expand[...].astype(F32).T.astype(BF16)
    w_project[...] = wprojt[...].astype(F32).T.astype(BF16)

    left = lax.rem(lon + sectors - 1, sectors)
    right = lax.rem(lon + 1, sectors)

    @pl.when(is_north)
    def _():
        mine = partner[:, pl.ds(pl.multiple_of(lon * TX, TX), TX)]
        from_left = partner[:, pl.ds(pl.multiple_of(left * TX, TX), TX)]
        from_right = partner[:, pl.ds(pl.multiple_of(right * TX, TX), TX)]
        near = jnp.zeros((1, TX), jnp.int32)
        for r in range(3 + TY, EXT):
            near = jnp.where(slot_lanes((1, TX), 4 * r, 3), turn(from_left, 4 * r - 125), near)
            near = jnp.where(slot_lanes((1, TX), 64 + 4 * r, 3), turn(from_right, 64 + 4 * r), near)
        wanted = jnp.concatenate([mine, near], axis=1)
        for s in range(sectors):
            col = lax.broadcasted_iota(jnp.int32, (TX, 2 * TX), 0) + s * TX
            onehot[s] = jnp.where(col == wanted, 1.0, 0.0).astype(BF16)
        col = lax.broadcasted_iota(jnp.int32, (TX, sectors * TX), 0) + lon * TX
        for b in range(7):
            beside = partner[...] if b == 3 else pltpu.roll(partner[...], (3 - b) % (sectors * TX), 1)
            onehot2[b * TX : (b + 1) * TX, :] = jnp.where(beside == col, 1.0, 0.0).astype(BF16)
        foldrecv[pl.ds(lon * (3 * C), 3 * C), :] = sendrows[3 * C :, :]

    def each_tile(body, height):
        def step(ct, carry):
            body(pl.ds(pl.multiple_of(ct * height, 8), height))
            return carry

        lax.fori_loop(0, C // height, step, 0)

    def own_body(cs):
        acc = conv_own(ext, kb, cs, False, [jnp.zeros((cs.size, 128), F32) for _ in range(TY)])
        for j in range(TY):
            conv[j, cs, :] = acc[j]

    each_tile(own_body, 16)

    def fill_halo(rows_r, edge_r, rows, edges, s):
        wait_bytes(rows_r, sems.at[2 * s + 1])
        wait_bytes(edge_r, sems.at[2 * s + 3])
        for k in range(3):
            rows[k] = jnp.where(is_south, 0.0, rows_r[k * C : (k + 1) * C, :].astype(F32))
            rows[11 + k] = jnp.where(
                is_north, 0.0, rows_r[(3 + k) * C : (4 + k) * C, :].astype(F32)
            )
        unpack_edges(edge_r, edges, is_south, is_north)

    fill_halo(recvrows, recvedge, ext, edge, 0)

    def south_body(cs):
        acc = [conv[j, cs, :] for j in range(TY)]
        acc = conv_edge(edge, kb, cs, False, acc, 0)
        acc = conv_halo(ext, kb, cs, False, acc, True, False)
        for j in range(TY):
            conv[j, cs, :] = acc[j]

    each_tile(south_body, 24)

    def mlp_body(m, carry):
        at = pl.ds(pl.multiple_of(m * 256, 256), 256)
        v = jnp.concatenate([conv[2 * m], conv[2 * m + 1]], axis=1).astype(BF16).astype(F32)
        center = v - jnp.mean(v, axis=0, keepdims=True)
        variance = jnp.mean(center * center, axis=0, keepdims=True)
        inv_std = lax.rsqrt(variance + 1e-06)
        normed = center * inv_std
        sc = (normed * gain_c).astype(BF16)
        scaled[:, at] = sc
        up = upstream[:, at]
        for h in range(0, HID, 256):
            pre = dot_nn(wexpt[h : h + 256, :], sc)
            gh = dot_nn(w_project[h : h + 256, :], up)
            half = 0.5 * (1.0 + lax.erf(pre * ROOT_HALF))
            hidden[h : h + 256, at] = (pre * half).astype(BF16)
            slope = half + pre * jnp.exp(-0.5 * pre * pre) * ROOT_TWOPI_INV
            gradpre[h : h + 256, at] = (gh * slope).astype(BF16)
        branch = dot_nn(wprojt[...], hidden[:, at]).astype(BF16).astype(F32)
        gs = dot_nn(w_expand[...], gradpre[:, at]) * gain_c
        gr = inv_std * (
            gs
            - jnp.mean(gs, axis=0, keepdims=True)
            - normed * jnp.mean(gs * normed, axis=0, keepdims=True)
        )
        gr = gr.astype(BF16).astype(F32)
        for n in range(2):
            half_at = slice(n * TX, (n + 1) * TX)
            j = 2 * m + n
            b = wet[pl.ds(j, 1), :] * scale_c * branch[:, half_at]
            nat[pl.ds(j, C, stride=TY), :] = ext[3 + j] + b
            gext[3 + j] = gr[:, half_at]
        return carry

    lax.fori_loop(0, TY // 4, mlp_body, 0)

    @pl.when(is_north)
    def _():
        wait_bytes(foldrecv.at[pl.ds(0, (sectors - 1) * 3 * C)], sems.at[5])
        corners = jnp.zeros((C, TX), F32)
        for k in range(3):
            acc = jnp.zeros((C, 2 * TX), F32)
            for s in range(sectors):
                base = s * 3 * C + (2 - k) * C
                acc = acc + dot_nn(foldrecv[base : base + C, :], onehot[s])
            ext[11 + k] = acc[:, :TX]
            at = 4 * (11 + k)
            here = slot_lanes((C, TX), at, 3) | slot_lanes((C, TX), 64 + at, 3)
            corners = jnp.where(here, acc[:, TX:], corners)
        fedge[...] = corners
        edge[...] = edge[...] + corners

        def corner_body(cs):
            acc = [None] * 5 + [conv[j, cs, :] for j in range(5, TY)]
            acc = conv_edge(fedge, kb, cs, False, acc, 5)
            for j in range(5, TY):
                conv[j, cs, :] = acc[j]

        each_tile(corner_body, 48)

    def north_body(cs):
        acc = [None] * 5 + [conv[j, cs, :] for j in range(5, TY)]
        acc = conv_halo(ext, kb, cs, False, acc, False, True)
        for j in range(5, TY):
            conv[j, cs, :] = acc[j]

    each_tile(north_body, 24)
    lax.fori_loop(TY // 4, TY // 2, mlp_body, 0)

    for k, j in enumerate((0, 1, 2, 5, 6, 7)):
        gsendrows[k * C : (k + 1) * C, :] = gext[3 + j].astype(BF16)

    ge = dot_nt(scaled[...], gradpre[...]).astype(BF16)
    gpt = dot_nt(upstream[...], hidden[...]).astype(BF16)
    blocks = HID // 128
    for b in range(blocks):
        part[b * C : (b + 1) * C, :] = ge[:, b * 128 : (b + 1) * 128]
        part[(blocks + b) * C : (blocks + b + 1) * C, :] = gpt[:, b * 128 : (b + 1) * 128]
    send(part.at[pl.ds((1 - core) * half_rows, half_rows)], besiderecv, 12, beside)
    out_field[...] = nat[...].astype(BF16)
    out_copy = pltpu.make_async_copy(out_field, out_nat, loads.at[0])
    out_copy.start()

    pack_edges(gext, gpacked)
    edge_messages(gpacked, gsendedge.at[0], gsendedge.at[1])
    wait_bytes(besiderecv, sems.at[25])
    half = part[pl.ds(pl.multiple_of(core * half_rows, 16), half_rows), :].astype(F32)
    halfsum[...] = (half + besiderecv[...].astype(F32)).astype(BF16)
    for o in range(1, sectors):
        to = peer(0, o)
        send(halfsum.at[pl.ds(to["lon"] * wch, wch)], partrecv.at[o - 1], 5, to)

    @pl.when(is_north)
    def _():
        here = pl.ds(pl.multiple_of(lon * TX, TX), TX)
        for o in range(1, sectors):
            send(gsendrows.at[pl.ds(3 * C, 3 * C)], foldrecv2.at[:, here], 6, peer(0, o))
        foldrecv2[:, here] = gsendrows[3 * C :, :]

    def gk_body(cs):
        lane = lax.broadcasted_iota(jnp.int32, (cs.size, 128), 1)
        x = ext[:, cs, :]
        g = gext[3 : 3 + TY, cs, :]
        terms = edge_terms(edge, cs)
        gp = gpacked[cs, :]
        beside = [turn(gp, 4 * a) for a in range(7)]
        for d in range(7):
            y = shifted(g, 6 - d)
            for a in range(7):
                v = jnp.sum(x[a : a + TY] * y, axis=0)
                if d < 3:
                    v = v + jnp.where(lane < 64, terms[d] * beside[a], 0.0)
                if d > 3:
                    v = v + jnp.where(lane >= 64, terms[6 - d] * beside[a], 0.0)
                gkparts[7 * a + d, cs, :] = v

    each_tile(gk_body, 8)
    lane = lax.broadcasted_iota(jnp.int32, (C, 128), 1)
    ones = jnp.ones((128, 128), BF16)
    res = jnp.zeros((C, 128), F32)
    for a in range(7):
        v = gkparts[7 * a : 7 * a + 7].reshape(7 * C, 128)
        hi = v.astype(BF16)
        lo = (v - hi.astype(F32)).astype(BF16)
        v = dot_nn(hi, ones) + dot_nn(lo, ones)
        for d in range(7):
            res = jnp.where(lane == 7 * a + d, v[d * C : (d + 1) * C], res)
    gk[...] = res
    for o in range(1, sectors):
        to = peer(0, o)
        send(gk.at[pl.ds(to["lon"] * kch, kch)], gkrecv.at[o - 1], 10, to)

    wait_bytes(partrecv, sems.at[11])
    own = halfsum[pl.ds(pl.multiple_of(lon * wch, 16), wch), :].astype(F32)
    for o in range(1, sectors):
        own = own + partrecv[o - 1].astype(F32)
    total[0:wch, :] = own
    if total.shape[0] > wch:
        total[wch:, :] = jnp.zeros((total.shape[0] - wch, 128), F32)
    for o in range(1, chips):
        to = peer(2 * o, 0)
        send(total.at[pl.ds((to["lat"] // 2) * piece, piece)], totalrecv.at[o - 1], 7, to)

    exchange(gsendrows, gsendedge, grecvrows, grecvedge, 3)

    wait_bytes(gkrecv, sems.at[21])
    own = gk[pl.ds(pl.multiple_of(lon * kch, 8), kch), :]
    for o in range(1, sectors):
        own = own + gkrecv[o - 1]
    gksum[...] = own
    for o in range(1, bands):
        send(gksum, gkall.at[o - 1], 11, peer(o, 0))

    mine = pl.ds(pl.multiple_of(chip * piece, 8), piece)
    acc = total[mine, :]
    wait_bytes(totalrecv, sems.at[15])
    for o in range(1, chips):
        acc = acc + totalrecv[o - 1]
    full[mine, :] = acc
    piece_at = pl.ds(chip * piece, piece)
    for o in range(1, chips):
        send(full.at[piece_at], full.at[piece_at], 8, peer(2 * o, 0))
    def adj_own_body(cs):
        acc = [cotr[j, cs, :] for j in range(TY)]
        acc = conv_own(gext, kb, cs, True, acc)
        for j in range(TY):
            conv[j, cs, :] = acc[j]

    each_tile(adj_own_body, 16)

    wait_bytes(full.at[pl.ds(0, (chips - 1) * piece)], sems.at[17])
    base = pl.multiple_of((core * sectors + lon) * fch, 16)
    final[pl.ds(base, wch), :] = full[0:wch, :].astype(BF16)
    wait_bytes(gkall, sems.at[23])
    own = gksum[...]
    for o in range(1, bands):
        own = own + gkall[o - 1]
    tail = jnp.zeros((fch - wch - kch, 128), F32)
    final[pl.ds(base + wch, fch - wch), :] = jnp.concatenate([own, tail], axis=0).astype(BF16)
    final_at = pl.ds((core * sectors + lon) * fch, fch)
    for o in range(1, sectors):
        send(final.at[final_at], final.at[final_at], 9, peer(0, o))

    fill_halo(grecvrows, grecvedge, gext, gedge, 3)

    def adj_halo_body(cs):
        acc = [conv[j, cs, :] for j in range(TY)]
        acc = conv_edge(gedge, kb, cs, True, acc, 0)
        acc = conv_halo(gext, kb, cs, True, acc, True, True)
        for j in range(TY):
            conv[j, cs, :] = acc[j]

    each_tile(adj_halo_body, 24)

    wait_bytes(final.at[pl.ds(0, (sectors - 1) * fch)], sems.at[19])
    half_at = pl.ds(core * (sectors * fch), sectors * fch)
    send(final.at[half_at], final.at[half_at], 13, beside)

    @pl.when(is_north)
    def _():
        wait_bytes(foldrecv2.at[:, pl.ds(0, (sectors - 1) * TX)], sems.at[13])
        for r in range(3):
            near = dot_nt(foldrecv2[r * C : (r + 1) * C, :], onehot2[...])
            for k in range(r + 1):
                acc = conv[7 - k]
                for b in range(7):
                    acc = acc + kb[7 * (6 + k - r) + b] * near[:, b * TX : (b + 1) * TX]
                conv[7 - k] = acc

    for j in range(TY):
        nat[pl.ds(j, C, stride=TY), :] = conv[j]
    grad_field[...] = nat[...].astype(BF16)
    grad_copy = pltpu.make_async_copy(grad_field, grad_nat, loads.at[1])
    grad_copy.start()

    wait_bytes(final.at[pl.ds(0, sectors * fch)], sems.at[27])
    sums_copy = pltpu.make_async_copy(final, sums_out, loads.at[2])
    sums_copy.start()

    out_copy.wait()
    grad_copy.wait()
    sums_copy.wait()
    wait_bytes(recvrows, sems.at[0])
    wait_bytes(recvedge, sems.at[2])
    wait_bytes(grecvrows, sems.at[6])
    wait_bytes(grecvedge, sems.at[8])
    wait_bytes(partrecv, sems.at[10])
    wait_bytes(gkrecv, sems.at[20])
    wait_bytes(besiderecv, sems.at[24])
    wait_bytes(final.at[pl.ds(0, sectors * fch)], sems.at[26])
    wait_bytes(gkall, sems.at[22])
    wait_bytes(totalrecv, sems.at[14])
    wait_bytes(totalrecv, sems.at[16])
    wait_bytes(final.at[pl.ds(0, (sectors - 1) * fch)], sems.at[18])

    @pl.when(is_north)
    def _():
        wait_bytes(foldrecv.at[pl.ds(0, (sectors - 1) * 3 * C)], sems.at[4])
        wait_bytes(foldrecv2.at[:, pl.ds(0, (sectors - 1) * TX)], sems.at[12])


def finish_kernel(
    sectors,
    out_nat,
    grad_nat,
    sums_in,
    out_field,
    grad_field,
    gkt,
    ge_out,
    gpt_out,
    gk,
    sums,
    fields,
    ge,
    gpt,
    sems,
):
    half_rows = WROWS // 2
    wch = half_rows // sectors
    kch = C // sectors
    fch = sums.shape[0] // (2 * sectors)
    load = pltpu.make_async_copy(sums_in, sums, sems.at[2])
    load.start()
    loads = [
        pltpu.make_async_copy(src, fields.at[n], sems.at[n])
        for n, src in enumerate((out_nat, grad_nat))
    ]
    for cp in loads:
        cp.start()
    load.wait()
    stores = []
    blocks = HID // 128
    for n, (dst, out) in enumerate(((ge, ge_out), (gpt, gpt_out))):
        for b in range(blocks):
            lanes = slice(b * 128, (b + 1) * 128)
            for r in range(0, C, PIECE):
                w = b * C + r
                at = (n * sectors + w // wch) * fch + w % wch
                dst[r : r + PIECE, lanes] = sums[at : at + PIECE, :].astype(F32)
        stores.append(pltpu.make_async_copy(dst, out, sems.at[3 + n]))
        stores[-1].start()
    for n, (cp, dst) in enumerate(zip(loads, (out_field, grad_field))):
        cp.wait()
        stores.append(pltpu.make_async_copy(fields.at[n], dst, sems.at[5 + n]))
        stores[-1].start()
    for n in range(sectors):
        at = n * fch + wch
        gk[n * kch : (n + 1) * kch, :] = sums[at : (n + 1) * fch, :].astype(F32)[:kch]
    gkt[...] = gk[...].T[:TAPS]
    for cp in stores:
        cp.wait()


def on_device(
    bands,
    sectors,
    state_field,
    depth_kernel,
    norm_gain,
    w_expand,
    w_project,
    layer_scale,
    cotangent,
    send_cells,
    send_count,
    fold_partner,
):
    wch = WROWS // 2 // sectors
    kch = C // sectors
    fch = wch + -(-kch // 16) * 16
    chips = bands // 2
    piece = -(-wch // (8 * chips)) * 8
    vmem = pl.BlockSpec(memory_space=pltpu.VMEM)
    hbm = pl.BlockSpec(memory_space=pltpu.HBM)
    smem = pl.BlockSpec(memory_space=pltpu.SMEM)
    sds = jax.ShapeDtypeStruct
    rows3 = pltpu.VMEM((6 * C, 128), BF16)
    edge = pltpu.VMEM((6, GC, 128), BF16)
    fold = pltpu.VMEM((sectors * 3 * C, 128), BF16)
    scratch = dict(
        nat=pltpu.VMEM((C * TY, 128), F32),
        ext=pltpu.VMEM((EXT, C, 128), F32),
        gext=pltpu.VMEM((EXT, C, 128), F32),
        edge=pltpu.VMEM((C, 128), F32),
        gedge=pltpu.VMEM((C, 128), F32),
        packed=pltpu.VMEM((C, 128), F32),
        gpacked=pltpu.VMEM((C, 128), F32),
        cotr=pltpu.VMEM((TY, C, 128), F32),
        conv=pltpu.VMEM((TY, C, 128), F32),
        upstream=pltpu.VMEM((C, CELLS), BF16),
        scaled=pltpu.VMEM((C, CELLS), BF16),
        hidden=pltpu.VMEM((HID, CELLS), BF16),
        gradpre=pltpu.VMEM((HID, CELLS), BF16),
        wexpt=pltpu.VMEM((HID, C), BF16),
        w_project=pltpu.VMEM((HID, C), BF16),
        wet=pltpu.VMEM((TY, TX), F32),
        kb=pltpu.VMEM((TAPS, C, 128), F32),
        fedge=pltpu.VMEM((C, 128), F32),
        gk=pltpu.VMEM((C, 128), F32),
        sendrows=rows3,
        sendedge=pltpu.VMEM((2, GC, 128), BF16),
        recvrows=rows3,
        recvedge=edge,
        gsendrows=rows3,
        gsendedge=pltpu.VMEM((2, GC, 128), BF16),
        grecvrows=rows3,
        grecvedge=edge,
        foldrecv=fold,
        foldrecv2=pltpu.VMEM((3 * C, sectors * TX), BF16),
        onehot=pltpu.VMEM((sectors, TX, 2 * TX), BF16),
        onehot2=pltpu.VMEM((7 * TX, sectors * TX), BF16),
        part=pltpu.VMEM((WROWS, 128), BF16),
        besiderecv=pltpu.VMEM((WROWS // 2, 128), BF16),
        halfsum=pltpu.VMEM((WROWS // 2, 128), BF16),
        partrecv=pltpu.VMEM((sectors - 1, wch, 128), BF16),
        gkparts=pltpu.VMEM((TAPS, C, 128), F32),
        gkrecv=pltpu.VMEM((sectors - 1, kch, 128), F32),
        gksum=pltpu.VMEM((kch, 128), F32),
        gkall=pltpu.VMEM((bands - 1, kch, 128), F32),
        total=pltpu.VMEM((chips * piece, 128), F32),
        totalrecv=pltpu.VMEM((chips - 1, piece, 128), F32),
        full=pltpu.VMEM((chips * piece, 128), F32),
        final=pltpu.VMEM((2 * sectors * fch, 128), BF16),
        sems=pltpu.SemaphoreType.DMA((28,)),
        state=pltpu.VMEM((C * TY, TX), BF16),
        cot=pltpu.VMEM((C * TY, TX), BF16),
        dkt=pltpu.VMEM((TAPS, C), F32),
        gain=pltpu.VMEM((1, C), F32),
        lscale=pltpu.VMEM((1, C), F32),
        w_expand=pltpu.VMEM((C, HID), BF16),
        wprojt=pltpu.VMEM((C, HID), BF16),
        cells=pltpu.VMEM((1, CELLS), jnp.int32),
        partner=pltpu.VMEM((1, sectors * TX), jnp.int32),
        out_field=pltpu.VMEM((C * TY, TX), BF16),
        grad_field=pltpu.VMEM((C * TY, TX), BF16),
        loads=pltpu.SemaphoreType.DMA((9,)),
    )
    out_nat, grad_nat, sums = pl.pallas_call(
        functools.partial(block_kernel, bands, sectors),
        out_shape=(
            sds((C * TY, TX), BF16),
            sds((C * TY, TX), BF16),
            sds((2 * sectors * fch, 128), BF16),
        ),
        in_specs=[hbm] * 8 + [smem] + [hbm],
        out_specs=(hbm, hbm, hbm),
        scratch_shapes=list(scratch.values()),
        compiler_params=pltpu.CompilerParams(
            collective_id=0, has_side_effects=True, vmem_limit_bytes=60 * 2**20
        ),
        name="block",
    )(
        state_field.reshape(C * TY, TX),
        cotangent.reshape(C * TY, TX),
        depth_kernel.T,
        norm_gain.reshape(1, C),
        layer_scale.reshape(1, C),
        w_expand,
        w_project.T,
        send_cells,
        send_count,
        fold_partner.reshape(1, sectors * TX),
    )
    out_field, grad_field, gkt, ge, gpt = pl.pallas_call(
        functools.partial(finish_kernel, sectors),
        out_shape=(
            sds((C * TY, TX), BF16),
            sds((C * TY, TX), BF16),
            sds((TAPS, C), F32),
            sds((C, HID), F32),
            sds((C, HID), F32),
        ),
        in_specs=[hbm, hbm, hbm],
        out_specs=(hbm, hbm, vmem, hbm, hbm),
        scratch_shapes=[
            pltpu.VMEM((C, 128), F32),
            pltpu.VMEM((2 * sectors * fch, 128), BF16),
            pltpu.VMEM((2, C * TY, TX), BF16),
            pltpu.VMEM((C, HID), F32),
            pltpu.VMEM((C, HID), F32),
            pltpu.SemaphoreType.DMA((7,)),
        ],
        compiler_params=pltpu.CompilerParams(vmem_limit_bytes=60 * 2**20),
        name="finish",
    )(out_nat, grad_nat, sums)
    return (
        out_field.reshape(C, TY, TX),
        grad_field.reshape(C, TY, TX),
        gkt.T,
        ge,
        gpt.T,
    )


def solution(mesh):
    return jax.shard_map(
        functools.partial(on_device, mesh.shape["lat"], mesh.shape["lon"]),
        mesh=mesh,
        in_specs=(
            P(None, "lat", "lon"),
            P(),
            P(),
            P(),
            P(),
            P(),
            P(None, "lat", "lon"),
            P("lat", "lon"),
            P("lat", "lon"),
            P(),
        ),
        out_specs=(P(None, "lat", "lon"), P(None, "lat", "lon"), P(), P(), P()),
        check_vma=False,
    )
```

```python
import functools

import jax
import jax.numpy as jnp
from jax import lax
from jax.experimental import pallas as pl
from jax.experimental.pallas import tpu as pltpu
from jax.sharding import PartitionSpec as P

MESH = pl.DeviceIdType.MESH
F32 = jnp.float32
BF16 = jnp.bfloat16
ROOT_HALF = 0.7071067811865476
ROOT_TWOPI_INV = 0.3989422804014327

C = 192
HID = 768
TY = 8
TX = 128
EXT = TY + 6
CELLS = TY * TX
TAPS = 49
GROUPS = 4
GC = C // GROUPS
WROWS = 2 * C * HID // 128
PIECE = 48


def dot_nn(a, b):
    return jnp.dot(a, b, preferred_element_type=F32)


def dot_nt(a, b):
    return lax.dot_general(a, b, (((1,), (1,)), ((), ())), preferred_element_type=F32)


def wait_bytes(ref, sem):
    pltpu.make_async_copy(ref, ref, sem).wait()


def column(row_ref):
    n = row_ref.shape[1]
    eye = lax.broadcasted_iota(jnp.int32, (n, n), 0) == lax.broadcasted_iota(
        jnp.int32, (n, n), 1
    )
    return jnp.sum(jnp.where(eye, row_ref[...], 0.0), axis=1, keepdims=True)


def slot_lanes(shape, base, n):
    lane = lax.broadcasted_iota(jnp.int32, shape, len(shape) - 1)
    return (lane >= base) & (lane < base + n)


def turn(x, shift):
    shift %= 128
    return pltpu.roll(x, shift, x.ndim - 1) if shift else x


def pack_edges(rows, packed):
    shape = (GC, 128)
    for q in range(GROUPS):
        at = slice(q * GC, (q + 1) * GC)
        p = jnp.zeros(shape, F32)
        for j in range(TY):
            x = rows[3 + j, at, :]
            p = jnp.where(slot_lanes(shape, 4 * j, 3), turn(x, 4 * j), p)
            p = jnp.where(slot_lanes(shape, 64 + 4 * j, 3), turn(x, 64 + 4 * j - 125), p)
        packed[at, :] = p


def edge_messages(packed, west, east):
    shape = (GC, 128)
    w = packed[0:GC, :]
    e = turn(w, 64)
    for q in range(1, GROUPS):
        x = packed[q * GC : (q + 1) * GC, :]
        here = slot_lanes(shape, 32 * q, 32)
        w = jnp.where(here, turn(x, 32 * q), w)
        e = jnp.where(here, turn(x, 32 * q - 64), e)
    west[...] = w.astype(BF16)
    east[...] = e.astype(BF16)


def unpack_edges(msgs, edge, is_south, is_north):
    shape = (GC, 128)
    lane = lax.broadcasted_iota(jnp.int32, shape, 1)
    within = jnp.bitwise_and(lane, 63)
    dead = (is_south & (within < 12)) | (is_north & (within >= 44))
    values = [msgs[n].astype(F32) for n in range(6)]
    for q in range(GROUPS):
        p = jnp.zeros(shape, F32)
        for side in range(2):
            for n, (at, width, j0) in enumerate(((0, 12, 5), (12, 32, 0), (44, 12, 0))):
                to = 64 * side + at
                x = turn(values[3 * side + n], to - 32 * q - 4 * j0)
                p = jnp.where(slot_lanes(shape, to, width), x, p)
        edge[q * GC : (q + 1) * GC, :] = jnp.where(dead, 0.0, p)


def shifted(x, d):
    sh = d - 3
    if sh == 0:
        return x
    lane = lax.broadcasted_iota(jnp.int32, x.shape, x.ndim - 1)
    x = jnp.where((lane >= sh) if sh > 0 else (lane < 128 + sh), x, 0.0)
    return turn(x, -sh)


def tap(a, d, reverse):
    t = 7 * a + d
    return TAPS - 1 - t if reverse else t


def conv_own(rows, kb, cs, reverse, acc):
    x = rows[3 : 3 + TY, cs, :]
    for d in range(7):
        y = shifted(x, d)
        for a in range(7):
            k = kb[tap(a, d, reverse), cs, :]
            for j in range(max(0, 3 - a), min(TY, 11 - a)):
                acc[j] = acc[j] + k * y[j + a - 3]
    return acc


def edge_terms(edge, cs):
    shape = (cs.size, 128)
    lane = lax.broadcasted_iota(jnp.int32, shape, 1)
    within = jnp.bitwise_and(lane, 3)
    left = lane < 64
    e = edge[cs, :]
    terms = [jnp.where(within < 3, e, 0.0)]
    for s in (1, 2):
        lf = jnp.where(left & (within <= 2 - s), turn(e, -s), 0.0)
        terms.append(
            jnp.where((lane >= 64) & (within >= s) & (within < 3), turn(e, s), lf)
        )
    return terms


def edge_sums(edge, kb, cs, reverse, offsets):
    left = slot_lanes((cs.size, 128), 0, 64)
    terms = edge_terms(edge, cs)
    total = None
    for a in offsets:
        y = None
        for s in range(3):
            lf = kb[tap(a, s, reverse), cs, :]
            rt = kb[tap(a, 6 - s, reverse), cs, :]
            k = jnp.where(left, lf, rt)
            y = k * terms[s] if y is None else y + k * terms[s]
        y = turn(y, -4 * a)
        total = y if total is None else total + y
    return total


def edge_row(total, j):
    west = jnp.where(slot_lanes(total.shape, 0, 3), turn(total, -4 * j), 0.0)
    return jnp.where(slot_lanes(total.shape, 125, 3), turn(total, 61 - 4 * j), west)


def conv_halo(rows, kb, cs, reverse, acc, south, north):
    if south:
        lo_rows = rows[0:3, cs, :]
    if north:
        hi_rows = rows[3 + TY :, cs, :]
    for d in range(7):
        if south:
            lo = shifted(lo_rows, d)
            for a in range(3):
                k = kb[tap(a, d, reverse), cs, :]
                for r in range(a, 3):
                    acc[r - a] = acc[r - a] + k * lo[r]
        if north:
            hi = shifted(hi_rows, d)
            for a in range(4, 7):
                k = kb[tap(a, d, reverse), cs, :]
                for r in range(0, a - 3):
                    acc[11 + r - a] = acc[11 + r - a] + k * hi[r]
    return acc


def conv_edge(edge, kb, cs, reverse, acc, first):
    total = edge_sums(edge, kb, cs, reverse, range(4 if first else 0, 7))
    for j in range(first, TY):
        acc[j] = acc[j] + edge_row(total, j)
    return acc


def block_kernel(
    bands,
    sectors,
    state_in,
    cot_in,
    dkt_in,
    gain_in,
    lscale_in,
    w_expand_in,
    wprojt_in,
    cells_in,
    counts,
    partner_in,
    out_nat,
    grad_nat,
    sums_out,
    nat,
    ext,
    gext,
    edge,
    gedge,
    packed,
    gpacked,
    cotr,
    conv,
    upstream,
    scaled,
    hidden,
    gradpre,
    wexpt,
    w_project,
    wet,
    kb,
    fedge,
    gk,
    sendrows,
    sendedge,
    recvrows,
    recvedge,
    gsendrows,
    gsendedge,
    grecvrows,
    grecvedge,
    foldrecv,
    foldrecv2,
    onehot,
    onehot2,
    part,
    geh,
    besiderecv,
    halfsum,
    partrecv,
    gkparts,
    gkrecv,
    gksum,
    gkall,
    total,
    totalrecv,
    full,
    final,
    sems,
    state,
    cot,
    dkt,
    gain,
    lscale,
    w_expand,
    wprojt,
    cells,
    partner,
    out_field,
    grad_field,
    loads,
):
    half_rows = WROWS // 2
    wch = half_rows // sectors
    kch = C // sectors
    fch = final.shape[0] // (2 * sectors)
    chips = bands // 2
    piece = totalrecv.shape[1]
    lat = lax.axis_index("lat")
    lon = lax.axis_index("lon")
    core = lax.rem(lat, 2)
    chip = lat // 2
    is_south = lat == 0
    is_north = lat == bands - 1

    def peer(dlat, dlon):
        return {
            "lat": lax.rem(lat + (dlat + bands), bands),
            "lon": lax.rem(lon + (dlon + sectors), sectors),
        }

    beside = {"lat": lat + 1 - 2 * core, "lon": lon}

    def send(src, dst, s, device):
        cp = pltpu.make_async_remote_copy(
            src_ref=src,
            dst_ref=dst,
            send_sem=sems.at[2 * s],
            recv_sem=sems.at[2 * s + 1],
            device_id=device,
            device_id_type=MESH,
        )
        cp.start()

    sources = (
        (state_in, state),
        (dkt_in, dkt),
        (cot_in, cot),
        (w_expand_in, w_expand),
        (wprojt_in, wprojt),
        (gain_in, gain),
        (lscale_in, lscale),
        (cells_in, cells),
        (partner_in, partner),
    )
    copies = [
        pltpu.make_async_copy(src, dst, loads.at[n]) for n, (src, dst) in enumerate(sources)
    ]
    for cp in copies:
        cp.start()

    barrier = pltpu.get_barrier_semaphore()
    peers = [(o, 0) for o in range(1, bands)] + [(0, o) for o in range(1, sectors)]
    peers += [(1, 1), (1, -1), (-1, 1), (-1, -1)]
    for dlat, dlon in peers:
        pl.semaphore_signal(barrier, inc=1, device_id=peer(dlat, dlon), device_id_type=MESH)

    copies[0].wait()
    nat[...] = state[...].astype(F32)
    for j in range(TY):
        ext[3 + j] = nat[pl.ds(j, C, stride=TY), :]
    for k, j in enumerate((0, 1, 2, 5, 6, 7)):
        sendrows[k * C : (k + 1) * C, :] = ext[3 + j].astype(BF16)
    pack_edges(ext, packed)
    edge_messages(packed, sendedge.at[0], sendedge.at[1])

    pl.semaphore_wait(barrier, len(peers))

    def exchange(rows_s, edge_s, rows_r, edge_r, s):
        for n, dlat in enumerate((1, 0, -1)):
            send(edge_s.at[1], edge_r.at[n], s + 1, peer(dlat, 1))
            send(edge_s.at[0], edge_r.at[3 + n], s + 1, peer(dlat, -1))
        send(rows_s.at[pl.ds(0, 3 * C)], rows_r.at[pl.ds(3 * C, 3 * C)], s, peer(-1, 0))
        send(rows_s.at[pl.ds(3 * C, 3 * C)], rows_r.at[pl.ds(0, 3 * C)], s, peer(1, 0))

    exchange(sendrows, sendedge, recvrows, recvedge, 0)

    @pl.when(is_north)
    def _():
        for o in range(1, sectors):
            send(
                sendrows.at[pl.ds(3 * C, 3 * C)],
                foldrecv.at[pl.ds(lon * (3 * C), 3 * C)],
                2,
                peer(0, o),
            )

    for cp in copies[1:]:
        cp.wait()

    seg = lax.broadcasted_iota(jnp.int32, (1, CELLS), 1)
    capacity = CELLS // bands
    filled = jnp.zeros((1, CELLS), jnp.int32)
    for p in range(bands):
        filled = jnp.where(seg // capacity == p, counts[0, p], filled)
    live = (seg % capacity) < filled
    row_of = jnp.right_shift(cells[...], 7)
    col_of = jnp.bitwise_and(cells[...], 127)
    in_row = (lax.broadcasted_iota(jnp.int32, (TY, CELLS), 0) == row_of) & live
    in_col = lax.broadcasted_iota(jnp.int32, (TX, CELLS), 0) == col_of
    wet[...] = dot_nt(
        jnp.where(in_row, 1.0, 0.0).astype(BF16), jnp.where(in_col, 1.0, 0.0).astype(BF16)
    )
    dkp = jnp.concatenate([dkt[...], jnp.zeros((128 - TAPS, C), F32)], axis=0).T
    for t in range(TAPS):
        kb[t] = jnp.broadcast_to(dkp[:, t : t + 1], (C, 128))

    gain_c = column(gain)
    scale_c = column(lscale)
    nat[...] = cot[...].astype(F32)
    for j in range(TY):
        x = nat[pl.ds(j, C, stride=TY), :]
        cotr[j] = x
        upstream[:, j * TX : (j + 1) * TX] = (wet[j : j + 1, :] * scale_c * x).astype(BF16)
    wexpt[...] = w_expand[...].astype(F32).T.astype(BF16)
    w_project[...] = wprojt[...].astype(F32).T.astype(BF16)

    left = lax.rem(lon + sectors - 1, sectors)
    right = lax.rem(lon + 1, sectors)

    @pl.when(is_north)
    def _():
        mine = partner[:, pl.ds(pl.multiple_of(lon * TX, TX), TX)]
        from_left = partner[:, pl.ds(pl.multiple_of(left * TX, TX), TX)]
        from_right = partner[:, pl.ds(pl.multiple_of(right * TX, TX), TX)]
        near = jnp.zeros((1, TX), jnp.int32)
        for r in range(3 + TY, EXT):
            near = jnp.where(slot_lanes((1, TX), 4 * r, 3), turn(from_left, 4 * r - 125), near)
            near = jnp.where(slot_lanes((1, TX), 64 + 4 * r, 3), turn(from_right, 64 + 4 * r), near)
        wanted = jnp.concatenate([mine, near], axis=1)
        for s in range(sectors):
            col = lax.broadcasted_iota(jnp.int32, (TX, 2 * TX), 0) + s * TX
            onehot[s] = jnp.where(col == wanted, 1.0, 0.0).astype(BF16)
        col = lax.broadcasted_iota(jnp.int32, (TX, sectors * TX), 0) + lon * TX
        for b in range(7):
            beside = partner[...] if b == 3 else pltpu.roll(partner[...], (3 - b) % (sectors * TX), 1)
            onehot2[b * TX : (b + 1) * TX, :] = jnp.where(beside == col, 1.0, 0.0).astype(BF16)
        foldrecv[pl.ds(lon * (3 * C), 3 * C), :] = sendrows[3 * C :, :]

    def each_tile(body, height):
        def step(ct, carry):
            body(pl.ds(pl.multiple_of(ct * height, 8), height))
            return carry

        lax.fori_loop(0, C // height, step, 0)

    def own_body(cs):
        acc = conv_own(ext, kb, cs, False, [jnp.zeros((cs.size, 128), F32) for _ in range(TY)])
        for j in range(TY):
            conv[j, cs, :] = acc[j]

    each_tile(own_body, 16)

    def fill_halo(rows_r, edge_r, rows, edges, s):
        wait_bytes(rows_r, sems.at[2 * s + 1])
        wait_bytes(edge_r, sems.at[2 * s + 3])
        for k in range(3):
            rows[k] = jnp.where(is_south, 0.0, rows_r[k * C : (k + 1) * C, :].astype(F32))
            rows[11 + k] = jnp.where(
                is_north, 0.0, rows_r[(3 + k) * C : (4 + k) * C, :].astype(F32)
            )
        unpack_edges(edge_r, edges, is_south, is_north)

    fill_halo(recvrows, recvedge, ext, edge, 0)

    def south_body(cs):
        acc = [conv[j, cs, :] for j in range(TY)]
        acc = conv_edge(edge, kb, cs, False, acc, 0)
        acc = conv_halo(ext, kb, cs, False, acc, True, False)
        for j in range(TY):
            conv[j, cs, :] = acc[j]

    each_tile(south_body, 24)

    def mlp_body(m, carry):
        at = pl.ds(pl.multiple_of(m * 256, 256), 256)
        v = jnp.concatenate([conv[2 * m], conv[2 * m + 1]], axis=1).astype(BF16).astype(F32)
        center = v - jnp.mean(v, axis=0, keepdims=True)
        variance = jnp.mean(center * center, axis=0, keepdims=True)
        inv_std = lax.rsqrt(variance + 1e-06)
        normed = center * inv_std
        sc = (normed * gain_c).astype(BF16)
        scaled[:, at] = sc
        up = upstream[:, at]
        for h in range(0, HID, 256):
            pre = dot_nn(wexpt[h : h + 256, :], sc)
            gh = dot_nn(w_project[h : h + 256, :], up)
            half = 0.5 * (1.0 + lax.erf(pre * ROOT_HALF))
            hidden[h : h + 256, at] = (pre * half).astype(BF16)
            slope = half + pre * jnp.exp(-0.5 * pre * pre) * ROOT_TWOPI_INV
            gradpre[h : h + 256, at] = (gh * slope).astype(BF16)
        branch = dot_nn(wprojt[...], hidden[:, at]).astype(BF16).astype(F32)
        gs = dot_nn(w_expand[...], gradpre[:, at]) * gain_c
        gr = inv_std * (
            gs
            - jnp.mean(gs, axis=0, keepdims=True)
            - normed * jnp.mean(gs * normed, axis=0, keepdims=True)
        )
        gr = gr.astype(BF16).astype(F32)
        for n in range(2):
            half_at = slice(n * TX, (n + 1) * TX)
            j = 2 * m + n
            b = wet[pl.ds(j, 1), :] * scale_c * branch[:, half_at]
            nat[pl.ds(j, C, stride=TY), :] = ext[3 + j] + b
            gext[3 + j] = gr[:, half_at]
        return carry

    lax.fori_loop(0, TY // 4, mlp_body, 0)

    early = CELLS // 2
    geh[0] = dot_nt(scaled[:, :early], gradpre[:, :early])
    geh[1] = dot_nt(upstream[:, :early], hidden[:, :early])

    @pl.when(is_north)
    def _():
        wait_bytes(foldrecv.at[pl.ds(0, (sectors - 1) * 3 * C)], sems.at[5])
        corners = jnp.zeros((C, TX), F32)
        for k in range(3):
            acc = jnp.zeros((C, 2 * TX), F32)
            for s in range(sectors):
                base = s * 3 * C + (2 - k) * C
                acc = acc + dot_nn(foldrecv[base : base + C, :], onehot[s])
            ext[11 + k] = acc[:, :TX]
            at = 4 * (11 + k)
            here = slot_lanes((C, TX), at, 3) | slot_lanes((C, TX), 64 + at, 3)
            corners = jnp.where(here, acc[:, TX:], corners)
        fedge[...] = corners
        edge[...] = edge[...] + corners

        def corner_body(cs):
            acc = [None] * 5 + [conv[j, cs, :] for j in range(5, TY)]
            acc = conv_edge(fedge, kb, cs, False, acc, 5)
            for j in range(5, TY):
                conv[j, cs, :] = acc[j]

        each_tile(corner_body, 48)

    def north_body(cs):
        acc = [None] * 5 + [conv[j, cs, :] for j in range(5, TY)]
        acc = conv_halo(ext, kb, cs, False, acc, False, True)
        for j in range(5, TY):
            conv[j, cs, :] = acc[j]

    each_tile(north_body, 24)
    lax.fori_loop(TY // 4, TY // 2, mlp_body, 0)

    for k, j in enumerate((0, 1, 2, 5, 6, 7)):
        gsendrows[k * C : (k + 1) * C, :] = gext[3 + j].astype(BF16)

    ge = (geh[0] + dot_nt(scaled[:, early:], gradpre[:, early:])).astype(BF16)
    gpt = (geh[1] + dot_nt(upstream[:, early:], hidden[:, early:])).astype(BF16)
    blocks = HID // 128
    for b in range(blocks):
        part[b * C : (b + 1) * C, :] = ge[:, b * 128 : (b + 1) * 128]
        part[(blocks + b) * C : (blocks + b + 1) * C, :] = gpt[:, b * 128 : (b + 1) * 128]
    send(part.at[pl.ds((1 - core) * half_rows, half_rows)], besiderecv, 12, beside)
    out_field[...] = nat[...].astype(BF16)
    out_copy = pltpu.make_async_copy(out_field, out_nat, loads.at[0])
    out_copy.start()

    pack_edges(gext, gpacked)
    edge_messages(gpacked, gsendedge.at[0], gsendedge.at[1])
    wait_bytes(besiderecv, sems.at[25])
    half = part[pl.ds(pl.multiple_of(core * half_rows, 16), half_rows), :].astype(F32)
    halfsum[...] = (half + besiderecv[...].astype(F32)).astype(BF16)
    for o in range(1, sectors):
        to = peer(0, o)
        send(halfsum.at[pl.ds(to["lon"] * wch, wch)], partrecv.at[o - 1], 5, to)

    @pl.when(is_north)
    def _():
        here = pl.ds(pl.multiple_of(lon * TX, TX), TX)
        for o in range(1, sectors):
            send(gsendrows.at[pl.ds(3 * C, 3 * C)], foldrecv2.at[:, here], 6, peer(0, o))
        foldrecv2[:, here] = gsendrows[3 * C :, :]

    def gk_body(cs):
        lane = lax.broadcasted_iota(jnp.int32, (cs.size, 128), 1)
        x = ext[:, cs, :]
        g = gext[3 : 3 + TY, cs, :]
        terms = edge_terms(edge, cs)
        gp = gpacked[cs, :]
        beside = [turn(gp, 4 * a) for a in range(7)]
        for d in range(7):
            y = shifted(g, 6 - d)
            for a in range(7):
                v = jnp.sum(x[a : a + TY] * y, axis=0)
                if d < 3:
                    v = v + jnp.where(lane < 64, terms[d] * beside[a], 0.0)
                if d > 3:
                    v = v + jnp.where(lane >= 64, terms[6 - d] * beside[a], 0.0)
                gkparts[7 * a + d, cs, :] = v

    each_tile(gk_body, 8)
    lane = lax.broadcasted_iota(jnp.int32, (C, 128), 1)
    ones = jnp.ones((128, 128), BF16)
    res = jnp.zeros((C, 128), F32)
    for a in range(7):
        v = gkparts[7 * a : 7 * a + 7].reshape(7 * C, 128)
        hi = v.astype(BF16)
        lo = (v - hi.astype(F32)).astype(BF16)
        v = dot_nn(hi, ones) + dot_nn(lo, ones)
        for d in range(7):
            res = jnp.where(lane == 7 * a + d, v[d * C : (d + 1) * C], res)
    gk[...] = res
    for o in range(1, sectors):
        to = peer(0, o)
        send(gk.at[pl.ds(to["lon"] * kch, kch)], gkrecv.at[o - 1], 10, to)

    wait_bytes(partrecv, sems.at[11])
    own = halfsum[pl.ds(pl.multiple_of(lon * wch, 16), wch), :].astype(F32)
    for o in range(1, sectors):
        own = own + partrecv[o - 1].astype(F32)
    total[0:wch, :] = own
    if total.shape[0] > wch:
        total[wch:, :] = jnp.zeros((total.shape[0] - wch, 128), F32)
    for o in range(1, chips):
        to = peer(2 * o, 0)
        send(total.at[pl.ds((to["lat"] // 2) * piece, piece)], totalrecv.at[o - 1], 7, to)

    exchange(gsendrows, gsendedge, grecvrows, grecvedge, 3)

    wait_bytes(gkrecv, sems.at[21])
    own = gk[pl.ds(pl.multiple_of(lon * kch, 8), kch), :]
    for o in range(1, sectors):
        own = own + gkrecv[o - 1]
    gksum[...] = own
    for o in range(1, bands):
        send(gksum, gkall.at[o - 1], 11, peer(o, 0))

    mine = pl.ds(pl.multiple_of(chip * piece, 8), piece)
    acc = total[mine, :]
    wait_bytes(totalrecv, sems.at[15])
    for o in range(1, chips):
        acc = acc + totalrecv[o - 1]
    full[mine, :] = acc
    piece_at = pl.ds(chip * piece, piece)
    for o in range(1, chips):
        send(full.at[piece_at], full.at[piece_at], 8, peer(2 * o, 0))
    def adj_own_body(cs):
        acc = [cotr[j, cs, :] for j in range(TY)]
        acc = conv_own(gext, kb, cs, True, acc)
        for j in range(TY):
            conv[j, cs, :] = acc[j]

    each_tile(adj_own_body, 16)

    wait_bytes(full.at[pl.ds(0, (chips - 1) * piece)], sems.at[17])
    base = pl.multiple_of((core * sectors + lon) * fch, 16)
    final[pl.ds(base, wch), :] = full[0:wch, :].astype(BF16)
    wait_bytes(gkall, sems.at[23])
    own = gksum[...]
    for o in range(1, bands):
        own = own + gkall[o - 1]
    tail = jnp.zeros((fch - wch - kch, 128), F32)
    final[pl.ds(base + wch, fch - wch), :] = jnp.concatenate([own, tail], axis=0).astype(BF16)
    final_at = pl.ds((core * sectors + lon) * fch, fch)
    for o in range(1, sectors):
        send(final.at[final_at], final.at[final_at], 9, peer(0, o))

    fill_halo(grecvrows, grecvedge, gext, gedge, 3)

    def adj_halo_body(cs):
        acc = [conv[j, cs, :] for j in range(TY)]
        acc = conv_edge(gedge, kb, cs, True, acc, 0)
        acc = conv_halo(gext, kb, cs, True, acc, True, True)
        for j in range(TY):
            conv[j, cs, :] = acc[j]

    each_tile(adj_halo_body, 24)

    wait_bytes(final.at[pl.ds(0, (sectors - 1) * fch)], sems.at[19])
    half_at = pl.ds(core * (sectors * fch), sectors * fch)
    send(final.at[half_at], final.at[half_at], 13, beside)

    @pl.when(is_north)
    def _():
        wait_bytes(foldrecv2.at[:, pl.ds(0, (sectors - 1) * TX)], sems.at[13])
        for r in range(3):
            near = dot_nt(foldrecv2[r * C : (r + 1) * C, :], onehot2[...])
            for k in range(r + 1):
                acc = conv[7 - k]
                for b in range(7):
                    acc = acc + kb[7 * (6 + k - r) + b] * near[:, b * TX : (b + 1) * TX]
                conv[7 - k] = acc

    for j in range(TY):
        nat[pl.ds(j, C, stride=TY), :] = conv[j]
    grad_field[...] = nat[...].astype(BF16)
    grad_copy = pltpu.make_async_copy(grad_field, grad_nat, loads.at[1])
    grad_copy.start()

    wait_bytes(final.at[pl.ds(0, sectors * fch)], sems.at[27])
    sums_copy = pltpu.make_async_copy(final, sums_out, loads.at[2])
    sums_copy.start()

    out_copy.wait()
    grad_copy.wait()
    sums_copy.wait()
    wait_bytes(recvrows, sems.at[0])
    wait_bytes(recvedge, sems.at[2])
    wait_bytes(grecvrows, sems.at[6])
    wait_bytes(grecvedge, sems.at[8])
    wait_bytes(partrecv, sems.at[10])
    wait_bytes(gkrecv, sems.at[20])
    wait_bytes(besiderecv, sems.at[24])
    wait_bytes(final.at[pl.ds(0, sectors * fch)], sems.at[26])
    wait_bytes(gkall, sems.at[22])
    wait_bytes(totalrecv, sems.at[14])
    wait_bytes(totalrecv, sems.at[16])
    wait_bytes(final.at[pl.ds(0, (sectors - 1) * fch)], sems.at[18])

    @pl.when(is_north)
    def _():
        wait_bytes(foldrecv.at[pl.ds(0, (sectors - 1) * 3 * C)], sems.at[4])
        wait_bytes(foldrecv2.at[:, pl.ds(0, (sectors - 1) * TX)], sems.at[12])


def finish_kernel(
    sectors,
    out_nat,
    grad_nat,
    sums_in,
    out_field,
    grad_field,
    gkt,
    ge_out,
    gpt_out,
    gk,
    sums,
    fields,
    ge,
    gpt,
    sems,
):
    half_rows = WROWS // 2
    wch = half_rows // sectors
    kch = C // sectors
    fch = sums.shape[0] // (2 * sectors)
    load = pltpu.make_async_copy(sums_in, sums, sems.at[2])
    load.start()
    loads = [
        pltpu.make_async_copy(src, fields.at[n], sems.at[n])
        for n, src in enumerate((out_nat, grad_nat))
    ]
    for cp in loads:
        cp.start()
    load.wait()
    stores = []
    blocks = HID // 128
    for n, (dst, out) in enumerate(((ge, ge_out), (gpt, gpt_out))):
        for b in range(blocks):
            lanes = slice(b * 128, (b + 1) * 128)
            for r in range(0, C, PIECE):
                w = b * C + r
                at = (n * sectors + w // wch) * fch + w % wch
                dst[r : r + PIECE, lanes] = sums[at : at + PIECE, :].astype(F32)
        stores.append(pltpu.make_async_copy(dst, out, sems.at[3 + n]))
        stores[-1].start()
    for n, (cp, dst) in enumerate(zip(loads, (out_field, grad_field))):
        cp.wait()
        stores.append(pltpu.make_async_copy(fields.at[n], dst, sems.at[5 + n]))
        stores[-1].start()
    for n in range(sectors):
        at = n * fch + wch
        gk[n * kch : (n + 1) * kch, :] = sums[at : (n + 1) * fch, :].astype(F32)[:kch]
    gkt[...] = gk[...].T[:TAPS]
    for cp in stores:
        cp.wait()


def on_device(
    bands,
    sectors,
    state_field,
    depth_kernel,
    norm_gain,
    w_expand,
    w_project,
    layer_scale,
    cotangent,
    send_cells,
    send_count,
    fold_partner,
):
    wch = WROWS // 2 // sectors
    kch = C // sectors
    fch = wch + -(-kch // 16) * 16
    chips = bands // 2
    piece = -(-wch // (8 * chips)) * 8
    vmem = pl.BlockSpec(memory_space=pltpu.VMEM)
    hbm = pl.BlockSpec(memory_space=pltpu.HBM)
    smem = pl.BlockSpec(memory_space=pltpu.SMEM)
    sds = jax.ShapeDtypeStruct
    rows3 = pltpu.VMEM((6 * C, 128), BF16)
    edge = pltpu.VMEM((6, GC, 128), BF16)
    fold = pltpu.VMEM((sectors * 3 * C, 128), BF16)
    scratch = dict(
        nat=pltpu.VMEM((C * TY, 128), F32),
        ext=pltpu.VMEM((EXT, C, 128), F32),
        gext=pltpu.VMEM((EXT, C, 128), F32),
        edge=pltpu.VMEM((C, 128), F32),
        gedge=pltpu.VMEM((C, 128), F32),
        packed=pltpu.VMEM((C, 128), F32),
        gpacked=pltpu.VMEM((C, 128), F32),
        cotr=pltpu.VMEM((TY, C, 128), F32),
        conv=pltpu.VMEM((TY, C, 128), F32),
        upstream=pltpu.VMEM((C, CELLS), BF16),
        scaled=pltpu.VMEM((C, CELLS), BF16),
        hidden=pltpu.VMEM((HID, CELLS), BF16),
        gradpre=pltpu.VMEM((HID, CELLS), BF16),
        wexpt=pltpu.VMEM((HID, C), BF16),
        w_project=pltpu.VMEM((HID, C), BF16),
        wet=pltpu.VMEM((TY, TX), F32),
        kb=pltpu.VMEM((TAPS, C, 128), F32),
        fedge=pltpu.VMEM((C, 128), F32),
        gk=pltpu.VMEM((C, 128), F32),
        sendrows=rows3,
        sendedge=pltpu.VMEM((2, GC, 128), BF16),
        recvrows=rows3,
        recvedge=edge,
        gsendrows=rows3,
        gsendedge=pltpu.VMEM((2, GC, 128), BF16),
        grecvrows=rows3,
        grecvedge=edge,
        foldrecv=fold,
        foldrecv2=pltpu.VMEM((3 * C, sectors * TX), BF16),
        onehot=pltpu.VMEM((sectors, TX, 2 * TX), BF16),
        onehot2=pltpu.VMEM((7 * TX, sectors * TX), BF16),
        part=pltpu.VMEM((WROWS, 128), BF16),
        geh=pltpu.VMEM((2, C, HID), F32),
        besiderecv=pltpu.VMEM((WROWS // 2, 128), BF16),
        halfsum=pltpu.VMEM((WROWS // 2, 128), BF16),
        partrecv=pltpu.VMEM((sectors - 1, wch, 128), BF16),
        gkparts=pltpu.VMEM((TAPS, C, 128), F32),
        gkrecv=pltpu.VMEM((sectors - 1, kch, 128), F32),
        gksum=pltpu.VMEM((kch, 128), F32),
        gkall=pltpu.VMEM((bands - 1, kch, 128), F32),
        total=pltpu.VMEM((chips * piece, 128), F32),
        totalrecv=pltpu.VMEM((chips - 1, piece, 128), F32),
        full=pltpu.VMEM((chips * piece, 128), F32),
        final=pltpu.VMEM((2 * sectors * fch, 128), BF16),
        sems=pltpu.SemaphoreType.DMA((28,)),
        state=pltpu.VMEM((C * TY, TX), BF16),
        cot=pltpu.VMEM((C * TY, TX), BF16),
        dkt=pltpu.VMEM((TAPS, C), F32),
        gain=pltpu.VMEM((1, C), F32),
        lscale=pltpu.VMEM((1, C), F32),
        w_expand=pltpu.VMEM((C, HID), BF16),
        wprojt=pltpu.VMEM((C, HID), BF16),
        cells=pltpu.VMEM((1, CELLS), jnp.int32),
        partner=pltpu.VMEM((1, sectors * TX), jnp.int32),
        out_field=pltpu.VMEM((C * TY, TX), BF16),
        grad_field=pltpu.VMEM((C * TY, TX), BF16),
        loads=pltpu.SemaphoreType.DMA((9,)),
    )
    out_nat, grad_nat, sums = pl.pallas_call(
        functools.partial(block_kernel, bands, sectors),
        out_shape=(
            sds((C * TY, TX), BF16),
            sds((C * TY, TX), BF16),
            sds((2 * sectors * fch, 128), BF16),
        ),
        in_specs=[hbm] * 8 + [smem] + [hbm],
        out_specs=(hbm, hbm, hbm),
        scratch_shapes=list(scratch.values()),
        compiler_params=pltpu.CompilerParams(
            collective_id=0, has_side_effects=True, vmem_limit_bytes=60 * 2**20
        ),
        name="block",
    )(
        state_field.reshape(C * TY, TX),
        cotangent.reshape(C * TY, TX),
        depth_kernel.T,
        norm_gain.reshape(1, C),
        layer_scale.reshape(1, C),
        w_expand,
        w_project.T,
        send_cells,
        send_count,
        fold_partner.reshape(1, sectors * TX),
    )
    out_field, grad_field, gkt, ge, gpt = pl.pallas_call(
        functools.partial(finish_kernel, sectors),
        out_shape=(
            sds((C * TY, TX), BF16),
            sds((C * TY, TX), BF16),
            sds((TAPS, C), F32),
            sds((C, HID), F32),
            sds((C, HID), F32),
        ),
        in_specs=[hbm, hbm, hbm],
        out_specs=(hbm, hbm, vmem, hbm, hbm),
        scratch_shapes=[
            pltpu.VMEM((C, 128), F32),
            pltpu.VMEM((2 * sectors * fch, 128), BF16),
            pltpu.VMEM((2, C * TY, TX), BF16),
            pltpu.VMEM((C, HID), F32),
            pltpu.VMEM((C, HID), F32),
            pltpu.SemaphoreType.DMA((7,)),
        ],
        compiler_params=pltpu.CompilerParams(vmem_limit_bytes=60 * 2**20),
        name="finish",
    )(out_nat, grad_nat, sums)
    return (
        out_field.reshape(C, TY, TX),
        grad_field.reshape(C, TY, TX),
        gkt.T,
        ge,
        gpt.T,
    )


def solution(mesh):
    return jax.shard_map(
        functools.partial(on_device, mesh.shape["lat"], mesh.shape["lon"]),
        mesh=mesh,
        in_specs=(
            P(None, "lat", "lon"),
            P(),
            P(),
            P(),
            P(),
            P(),
            P(None, "lat", "lon"),
            P("lat", "lon"),
            P("lat", "lon"),
            P(),
        ),
        out_specs=(P(None, "lat", "lon"), P(None, "lat", "lon"), P(), P(), P()),
        check_vma=False,
    )
```
